32 devices in a mesh: band: 4 (over z), ty: 4 (over y, core), tx: 2 (over x).
Axes of the slice: x: 2, y: 2, z: 4, core: 2. Of those that a mesh axis runs over, the one named last changes fastest.
Arguments:
- dirty: float32 [8, 1024, 512], P('band', 'ty', 'tx'), may hold values from -6 to 6
- psf: bfloat16 [8, 20, 2304], P('band'), may hold values from -4 to 4
- comp_tile: int32 [1024, 1], P(('ty', 'tx')), may hold values from 0 to 7; in each aligned block of 128 rows (0 to 127, 128 to 255, ...) at most 32 rows name the same one
- comp_offset: int32 [1024, 2], P(('ty', 'tx')), may hold values from 0 to 255
- comp_scale: int32 [1024], P(('ty', 'tx')), may hold values from 0 to 4
- comp_amp: float32 [1024, 4], P(('ty', 'tx')), may hold values from -6 to 6
- fit_weight: float32 [8, 4], P('band'), may hold values from -5 to 5
Outputs:
- residual: float32 [8, 1024, 512], P('band', 'ty', 'tx')
- taylor_fit: float32 [4, 1024, 512], P('band', 'ty', 'tx')
The draws below stay inside these ranges and needn't reach their ends.
Inputs may be any that keep to these rules, and one draw needn't show every extreme that they name: `comp_tile`: the 128 components of one device name at most 32 components for one tile, and exactly 32 for some tile on some device.
All inputs are finite; a program needn't handle non-finite values.
Results may differ from the reference program's by a relative error of at most 0.0022.
Values may be sent and summed in bfloat16 or wider, within the bound.
No kernel may reach another device: no remote copies, remote signals or barrier semaphores. Data moves between devices by JAX's collectives and lax.ppermute only.
A program may use at most 64 MiB of HBM per device.

```python
import math
import jax
import jax.numpy as jnp
import numpy as np
from jax import lax

BANDS = 8
TAYLOR = 4
SCALES = 5
PATCH = 48
TILE = 256
K_DEV = 128
CAP = 32
COMPS = 1024
NY = 1024
NX = 512
N_TY = 4
N_TX = 2


def plant(array, key, least, top_value):
    longest = array.shape.index(max(array.shape))
    spots = []
    for shift in (0, 1):
        where = [jax.random.randint(jax.random.fold_in(key, axis), (), 0, length) for axis, length in enumerate(array.shape)]
        where[longest] = (where[longest] + shift) % array.shape[longest]
        spots.append(tuple(where))
    return array.at[spots[0]].set(least).at[spots[1]].set(top_value)


def levels(stream_key, dims, split, least, high):
    level, own = 1.0, jax.random.fold_in(stream_key, 6)
    for dim, shards_of in split:
        steps = jnp.exp(jax.random.uniform(jax.random.fold_in(own, dim), (shards_of,), jnp.float32, least / len(split), high / len(split)))
        level = level * jnp.repeat(steps, dims[dim] // shards_of).reshape([-1 if axis == dim else 1 for axis in range(len(dims))])
    return level


def shared_out(key, own, number, rows, amount, top, reach, skew):
    sequence = jax.random.permutation(key, amount)
    heavy_load, usual = load_shares(amount, rows * top, reach, skew, True), load_shares(amount, rows * top, reach, skew, False)
    places = jnp.arange(amount)

    def named(sizes, offset_by):
        used = int((sizes > 0).sum())
        fixed = max(1, used // 4)
        moved = fixed + (places - fixed + offset_by * (used - fixed)) % max(1, amount - fixed)
        return jnp.zeros((amount,), jnp.int32).at[sequence[jnp.where(places < fixed, places, moved)]].set(jnp.asarray(sizes, jnp.int32))

    sizes = jnp.where(number % 4 == 0, named(heavy_load, number // 4), named(usual, number - number // 4 - 1))
    mixed = jax.random.permutation(jax.random.fold_in(own, 3), amount)
    source_of, taker = mixed[0:amount // 2 * 2:2], mixed[1:amount // 2 * 2:2]
    room = jnp.minimum(sizes[source_of] - 1, reach - sizes[taker]) // 2
    room = jnp.where((source_of == sequence[0]) | (taker == sequence[0]) | (sizes[taker] == 0), 0, jnp.maximum(room, 0))
    moved = jax.random.randint(jax.random.fold_in(own, 4), (amount // 2,), 0, 1 << 20) % (room + 1)
    sizes = sizes.at[source_of].add(-moved).at[taker].add(moved)
    members = jnp.searchsorted(jnp.cumsum(sizes), jnp.arange(rows * top), side="right").astype(jnp.int32)
    table = members.reshape(top, rows).T
    table = table[jax.random.permutation(jax.random.fold_in(own, 1), rows)]
    offset_by = jax.random.randint(jax.random.fold_in(own, 2), (rows, 1), 0, top)
    return jnp.take_along_axis(table, (jnp.arange(top)[None, :] + offset_by) % top, axis=1)


def load_shares(number_of, total, most, slope, full):
    weights = [(1 << 20) // math.isqrt(grade ** slope) + 1 for grade in range(1, number_of + 1)]
    largest = most if full else min(most, max(-(-total // number_of), total * weights[0] // sum(weights)))
    least = 1 if total - largest >= number_of - 1 else 0
    counts, rest = [largest] + [least] * (number_of - 1), total - largest - least * (number_of - 1)
    while rest > 0:
        free = [i for i in range(1, number_of) if counts[i] < largest] or [i for i in range(1, number_of) if counts[i] < most]
        pool, left = sum([weights[i] for i in free]), rest
        for i in free:
            addition = min(most - counts[i], max(1, left * weights[i] // pool), rest)
            counts[i] = counts[i] + addition
            rest = rest - addition
    return np.array(counts)


def centred(key, dims, scale, limit, shards=(), kind=jnp.bfloat16):
    array = jax.random.normal(key, dims, jnp.float32) * scale
    if len(shards) > 0:
        array = levels(key, dims, shards, -0.22, 0.18) * array
    return jnp.clip(array, min=-limit, max=limit).astype(kind)


def setup_inputs(seed: int = 0) -> dict:
    seeds = jax.random.split(jax.random.key(seed), 8)
    dirty = centred(seeds[0], (BANDS, NY, NX), 1.0, 6.0, ((0, 4), (1, 4), (2, 2)), jnp.float32)
    psf = centred(seeds[1], (BANDS, TAYLOR * SCALES, PATCH * PATCH), 0.25, 4.0, ((0, 4),))
    comp_tile_keys = jax.random.split(jax.random.fold_in(seeds[2], 1), COMPS // K_DEV)
    comp_tile_turns = jax.random.permutation(jax.random.fold_in(seeds[2], 3), COMPS // K_DEV)
    comp_tile = jax.vmap(lambda own, number: shared_out(jax.random.fold_in(seeds[2], 2), own, number, K_DEV, N_TY * N_TX, 1, CAP, 2))(comp_tile_keys, comp_tile_turns).reshape((COMPS, 1))
    comp_offset = plant(jax.random.randint(seeds[3], (COMPS, 2), 0, TILE), jax.random.fold_in(seeds[3], 1), 0, TILE - 1).astype(jnp.int32)
    comp_scale = plant(jax.random.randint(seeds[4], (COMPS,), 0, SCALES), jax.random.fold_in(seeds[4], 1), 0, SCALES - 1).astype(jnp.int32)
    comp_amp = centred(seeds[5], (COMPS, TAYLOR), 1.0, 6.0, ((0, 8),), jnp.float32)
    fit_weight = centred(seeds[6], (BANDS, TAYLOR), 0.35, 5.0, ((0, 4),), jnp.float32)
    return {"dirty": dirty, "psf": psf, "comp_tile": comp_tile, "comp_offset": comp_offset, "comp_scale": comp_scale, "comp_amp": comp_amp, "fit_weight": fit_weight}


def reference(dirty, psf, comp_tile, comp_offset, comp_scale, comp_amp, fit_weight):
    tiles = comp_tile[:, 0]
    row_start = (tiles // N_TX) * TILE + comp_offset[:, 0]
    col_start = (tiles % N_TX) * TILE + comp_offset[:, 1]
    select = (comp_scale[:, None] == jnp.arange(SCALES, dtype=jnp.int32)[None, :]).astype(jnp.float32)
    coef = (comp_amp[:, :, None] * select[:, None, :]).reshape(COMPS, TAYLOR * SCALES)
    span = jnp.arange(PATCH, dtype=jnp.int32)
    rows = row_start[:, None, None] + span[None, :, None]
    cols = col_start[:, None, None] + span[None, None, :]

    def one_band(pair):
        psf_band, dirty_band = pair
        patches = jnp.dot(coef, psf_band.astype(jnp.float32), precision=lax.Precision.HIGHEST)
        patches = lax.optimization_barrier(patches.astype(jnp.bfloat16)).astype(jnp.float32)
        patches = patches.reshape(COMPS, PATCH, PATCH)
        model = jnp.zeros((NY + PATCH, NX + PATCH), jnp.float32).at[rows, cols].add(patches)
        return dirty_band - model[:NY, :NX]

    residual = lax.map(one_band, (psf, dirty))
    taylor_fit = jnp.einsum("bt,byx->tyx", fit_weight, residual, precision=lax.Precision.HIGHEST)
    return residual, taylor_fit
```

```python
import math, functools
import jax, jax.numpy as jnp
from jax import lax
from jax.experimental import pallas as pl
from jax.experimental.pallas import tpu as pltpu
from jax.sharding import PartitionSpec as P
LANES=128; HALF=64; U=4

def pick(flat, first, dest, lane):
    c, off = divmod(first, LANES)
    a = flat[:, c*LANES:(c+1)*LANES]
    if off + 48 > LANES:
        a = jnp.where(lane >= off, a, flat[:, (c+1)*LANES:(c+2)*LANES])
    sh = (dest - off) % LANES
    return pltpu.roll(a, sh, 1) if sh else a

def pack_kernel(psf_ref, out_ref, *, patch):
    kk = psf_ref.shape[1]
    b0 = psf_ref[0].astype(jnp.float32); b1 = psf_ref[1].astype(jnp.float32)
    lane = lax.broadcasted_iota(jnp.int32, (kk, LANES), 1)
    for u in range(patch):
        v = jnp.where(lane < HALF, pick(b0, u*patch, 0, lane), pick(b1, u*patch, HALF, lane))
        out_ref[pl.ds(u, kk, stride=patch), :] = jnp.where(lane % HALF < patch, v, 0.0)

def pack_half_kernel(psi_ref, out_ref, *, patch):
    kk = psi_ref.shape[0]
    b0 = psi_ref[...]
    h = patch//2
    lane = lax.broadcasted_iota(jnp.int32, (kk, LANES), 1)
    for u in range(h):
        v = jnp.where(lane < HALF, pick(b0, u*patch, 0, lane), pick(b0, (u+h)*patch, HALF, lane))
        out_ref[pl.ds(u, kk, stride=h), :] = jnp.where(lane % HALF < patch, v, 0.0)

def render_kernel(feat_ref, ints_ref, amps_ref, g_ref, gt_ref, dirty_ref, res_ref, tay_ref,
                  ints_s, amps_s, list_v, list_s, acc, acct, sems, *, patch, tile, taylor, scales):
    rows = tile + 2*patch
    S = feat_ref.shape[1]
    c1 = pltpu.make_async_copy(ints_ref, ints_s, sems.at[0]); c1.start()
    c2 = pltpu.make_async_copy(amps_ref, amps_s, sems.at[1]); c2.start()
    for j in range(1, acc.shape[0]//rows - 1):
        acc[pl.ds(j*rows+patch, tile), :] = jnp.zeros((tile, LANES), jnp.float32)
        acct[pl.ds(j*rows+patch-patch//2, tile+patch//2), :] = jnp.zeros((tile+patch//2, LANES), jnp.float32)
    rr = feat_ref[0]; cc = feat_ref[1]
    mask = (rr > -patch) & (rr < tile) & (cc > -patch) & (cc < tile)
    mf = jnp.where(mask, 1.0, 0.0)
    i0 = lax.broadcasted_iota(jnp.int32, (LANES, LANES), 0)
    i1 = lax.broadcasted_iota(jnp.int32, (LANES, LANES), 1)
    upper = jnp.where(i0 < i1, 1.0, 0.0).astype(jnp.bfloat16)
    ones = jnp.ones((LANES, LANES), jnp.bfloat16)
    sl = jnp.where(lax.broadcasted_iota(jnp.int32, (S, S), 1) < lax.broadcasted_iota(jnp.int32, (S, S), 0), 1.0, 0.0).astype(jnp.bfloat16)
    mb = mf.astype(jnp.bfloat16)
    f32 = jnp.float32
    before = jnp.dot(sl, mb, preferred_element_type=f32)
    rank = jnp.dot(mb, upper, preferred_element_type=f32) + jnp.dot(before.astype(jnp.bfloat16), ones, preferred_element_type=f32)
    total = jnp.dot(jnp.ones((8, S), jnp.bfloat16), mb, preferred_element_type=f32)
    total = jnp.dot(total.astype(jnp.bfloat16), ones, preferred_element_type=f32)
    rank_i = jnp.where(mask, rank, -1.0).astype(jnp.int32)
    lo = rank_i & (LANES-1)
    hi = jnp.where(mask, rank_i >> 7, -1)
    lane_row = lax.broadcasted_iota(jnp.int32, (S, LANES), 1).astype(f32)
    srow = lax.broadcasted_iota(jnp.int32, (S, LANES), 0)
    flat_i = jnp.zeros((S, LANES), f32); flat_d = jnp.zeros((S, LANES), f32)
    for d in range(S):
        hit = (hi[d:d+1, :] == srow)
        onehot = jnp.where(lo[d:d+1, :] == i0, 1.0, 0.0).astype(jnp.bfloat16)
        lhs = jnp.concatenate([jnp.where(hit, lane_row, 0.0), jnp.where(hit, float(d), 0.0)], 0).astype(jnp.bfloat16)
        got = lax.dot_general(lhs, onehot, (((1,), (1,)), ((), ())), preferred_element_type=f32)
        flat_i += got[:S]; flat_d += got[S:]
    list_v[0:S, :] = flat_d.astype(jnp.int32)*LANES + flat_i.astype(jnp.int32)
    list_v[S:S+8, :] = total.astype(jnp.int32)
    c3 = pltpu.make_async_copy(list_v, list_s, sems.at[2]); c3.start()
    c1.wait(); c2.wait(); c3.wait()
    n = list_s[S, 0]
    lane = lax.broadcasted_iota(jnp.int32, (1, LANES), 1)
    lane_half = lane & (HALF-1)
    h = patch//2

    def gen(i):
        idx = list_s[i >> 7, i & 127]
        idx = jnp.where(i < n, idx, S*LANES)
        row = (idx >> 7)*4; col = idx & 127
        base = ints_s[row, col]; shift = ints_s[row+1, col]; sc = ints_s[row+2, col]
        a = [amps_s[row+t, col] for t in range(taylor)]
        p = None; q = None
        for t in range(taylor):
            k = t*scales + sc
            g = g_ref[pl.ds(pl.multiple_of(k*patch, 8), patch), :]
            gt = gt_ref[pl.ds(pl.multiple_of(k*h, 8), h), :]
            p = a[t]*g if p is None else p + a[t]*g
            q = a[t]*gt if q is None else q + a[t]*gt
        p = p.astype(jnp.bfloat16).astype(f32)
        return (pltpu.roll(p, shift, 1), pltpu.roll(q, shift, 1), base, shift & (HALF-1))

    def put(item):
        p, q, base, w = item
        first = lane_half >= w
        for ref, val, hh in ((acc, p, patch), (acct, q, h)):
            b1 = pl.ds(base, hh); b2 = pl.ds(base + rows, hh)
            ref[b1, :] = ref[b1, :] + jnp.where(first, val, 0.0)
            ref[b2, :] = ref[b2, :] + jnp.where(first, 0.0, val)

    def step(i, carry):
        nxt = tuple(gen((i+1)*U + k) for k in range(U))
        for item in carry: put(item)
        return nxt
    last = lax.fori_loop(0, (n + U - 1)//U, step, tuple(gen(k) for k in range(U)))

    left = lax.broadcasted_iota(jnp.int32, (tile, LANES), 1) < HALF
    for c in range(tile//LANES):
        j = 2*c + 1
        def get(ref, jj, r0): return ref[pl.ds(jj*rows + r0, tile), :]
        x = get(acc, j, patch); y = get(acc, j+1, patch)
        res_ref[0, :, c*LANES:(c+1)*LANES] = dirty_ref[0, :, c*LANES:(c+1)*LANES] - jnp.where(left, x, y)
        res_ref[1, :, c*LANES:(c+1)*LANES] = dirty_ref[1, :, c*LANES:(c+1)*LANES] - pltpu.roll(jnp.where(left, y, x), HALF, 1)
        up = jnp.where(left, get(acct, j, patch), get(acct, j+1, patch))
        low = pltpu.roll(jnp.where(left, get(acct, j+1, patch-h), get(acct, j, patch-h)), HALF, 1)
        tay_ref[0, :, c*LANES:(c+1)*LANES] = up + low

def pack(psf, patch):
    return pl.pallas_call(functools.partial(pack_kernel, patch=patch),
        out_shape=jax.ShapeDtypeStruct((psf.shape[1]*patch, LANES), jnp.float32))(psf)
def pack_half(psi, patch):
    return pl.pallas_call(functools.partial(pack_half_kernel, patch=patch),
        out_shape=jax.ShapeDtypeStruct((psi.shape[0]*(patch//2), LANES), jnp.float32))(psi)

def render(feats, g, gt, dirty, r0, c0, *, patch, taylor, scales):
    tile = dirty.shape[1]; rows = tile + 2*patch; S = feats.shape[0]
    tiles = tile//HALF + 2
    rr = feats[:, 0] - r0; cc = feats[:, 1] - c0
    fz = jnp.stack([rr, cc])
    ri = jnp.clip(rr.astype(jnp.int32), -patch, tile) + patch
    ci = jnp.clip(cc.astype(jnp.int32), -HALF, tile - 1)
    base = ((ci + HALF)//HALF)*rows + ri
    base = jnp.minimum(base, (tiles-1)*rows - patch)
    ints = jnp.stack([base, ci & (LANES-1), feats[:, 2].astype(jnp.int32), jnp.zeros_like(base)], 1)
    amps = feats[:, 3:3+taylor]
    ints = jnp.concatenate([ints, jnp.zeros((1,)+ints.shape[1:], jnp.int32)], 0).reshape(-1, LANES)
    amps = jnp.concatenate([amps, jnp.zeros((1,)+amps.shape[1:], jnp.float32)], 0).reshape(-1, LANES)
    V = pl.BlockSpec(memory_space=pltpu.VMEM)
    f32 = jnp.float32
    return pl.pallas_call(
        functools.partial(render_kernel, patch=patch, tile=tile, taylor=taylor, scales=scales),
        out_shape=(jax.ShapeDtypeStruct(dirty.shape, f32), jax.ShapeDtypeStruct((1,)+dirty.shape[1:], f32)),
        in_specs=[V]*6, out_specs=(V, V),
        scratch_shapes=[pltpu.SMEM(ints.shape, jnp.int32), pltpu.SMEM(amps.shape, f32),
            pltpu.VMEM((S+8, LANES), jnp.int32), pltpu.SMEM((S+8, LANES), jnp.int32),
            pltpu.VMEM((tiles*rows, LANES), f32), pltpu.VMEM((tiles*rows, LANES), f32),
            pltpu.SemaphoreType.DMA((3,))],
        compiler_params=pltpu.CompilerParams(vmem_limit_bytes=32*1024*1024),
    )(fz, ints, amps, g, gt, dirty)


def doubled(value, axes, size):
    held = value[None]
    bit = 1
    while bit < size:
        other = lax.ppermute(held, axes, [(i, i ^ bit) for i in range(size)])
        held = jnp.concatenate([held, other], 0)
        bit *= 2
    return held


def per_device(dirty, psf, comp_tile, comp_offset, comp_scale, comp_amp, fit_weight):
    bands_here, tile = dirty.shape[0], dirty.shape[1]
    patch = math.isqrt(psf.shape[2])
    taylor = comp_amp.shape[1]
    scales = psf.shape[1] // taylor
    n_ty, n_tx, n_band = lax.axis_size("ty"), lax.axis_size("tx"), lax.axis_size("band")
    ty, tx, me = lax.axis_index("ty"), lax.axis_index("tx"), lax.axis_index("band")
    f32 = jnp.float32
    where_tile = comp_tile[:, 0]
    row = (where_tile // n_tx) * tile + comp_offset[:, 0]
    col = (where_tile % n_tx) * tile + comp_offset[:, 1]
    ints = jnp.stack([row, col, comp_scale], 0).astype(f32)
    feats = jnp.concatenate([ints, comp_amp.T, jnp.zeros((8 - 3 - taylor, row.shape[0]), f32)], 0)
    lift = 2.0 ** math.floor(math.log2(60000.0 / (bands_here * 30.0)))

    def weighted(values, step):
        w = lax.dynamic_slice_in_dim(fit_weight, me ^ step, 1, 1)[:, 0]
        total = w[0] * values[0].astype(f32)
        for b in range(1, bands_here):
            total = total + w[b] * values[b].astype(f32)
        return total

    def summed(values):
        total = weighted(values, 0)
        for step in range(1, n_band):
            part = (weighted(values, step) * lift).astype(jnp.float16)
            got = lax.ppermute(part, "band", [(i, i ^ step) for i in range(n_band)])
            total = total + got.astype(f32) * (1.0 / lift)
        return total

    everyone = doubled(feats, ("ty", "tx"), n_ty * n_tx)
    psi = summed(psf)
    dirty_fit = summed(dirty)
    residual, model_fit = render(
        everyone, pack(psf, patch), pack_half(psi, patch), dirty,
        (ty * tile).astype(f32), (tx * tile).astype(f32),
        patch=patch, taylor=taylor, scales=scales)
    return residual, dirty_fit[None] - model_fit


def solution(mesh):
    return jax.shard_map(
        per_device,
        mesh=mesh,
        in_specs=(
            P("band", "ty", "tx"),
            P("band", None, None),
            P(("ty", "tx"), None),
            P(("ty", "tx"), None),
            P(("ty", "tx")),
            P(("ty", "tx"), None),
            P("band", None),
        ),
        out_specs=(P("band", "ty", "tx"), P("band", "ty", "tx")),
        check_vma=False,
    )
```

```python
import functools
import math
import jax
import jax.numpy as jnp
from jax import lax
from jax.experimental import pallas as pl
from jax.experimental.pallas import tpu as pltpu
from jax.sharding import PartitionSpec as P

LANES = 128
HALF = 64
U = 16
F32, BF16, I32 = jnp.float32, jnp.bfloat16, jnp.int32


def vmem():
    return pl.BlockSpec(memory_space=pltpu.VMEM)


def prep_kernel(w_hbm, tile_hbm, offset_hbm, scale_hbm, amp_hbm, dirty_hbm, psf_hbm,
                feat_ref, dpart_ref, ppart_ref, plane_ref,
                w_ref, tile_ref, offset_ref, scale_ref, amp_ref, dirty_ref, psf_ref, pairs, psi, sems, *,
                me, half, n_tx, n_band):
    copies = [pltpu.make_async_copy(src, dst, sems.at[i]) for i, (src, dst) in enumerate((
        (psf_hbm, psf_ref), (w_hbm, w_ref), (tile_hbm, tile_ref), (offset_hbm, offset_ref),
        (scale_hbm, scale_ref), (amp_hbm, amp_ref), (dirty_hbm, dirty_ref)))]
    for copy in copies:
        copy.start()
    bands, side = dirty_ref.shape[0], dirty_ref.shape[1]
    kk, flat = psf_ref.shape[0], psf_ref.shape[2]
    taylor = amp_ref.shape[0]
    me, half = me(), half()
    part, deep = kk // 2, -(-kk // 8) * 8
    copies[0].wait()
    copies[1].wait()
    for c in range(flat // LANES):
        cols = slice(c * LANES, (c + 1) * LANES)
        top = c * bands * kk
        for k in range(kk):
            pairs[top + bands * k:top + bands * (k + 1), :] = psf_ref[k, :, cols].astype(F32)
    planes = {}
    for c in range(flat // LANES):
        for b in range(bands):
            planes[b, c] = pairs[pl.ds(c * bands * kk + b, kk, stride=bands), :]
            plane_ref[b, :, c * LANES:(c + 1) * LANES] = planes[b, c]
    for step in range(n_band):
        to = me ^ step
        for c in range(flat // LANES):
            total = w_ref[0, to] * planes[0, c]
            for b in range(1, bands):
                total = total + w_ref[b, to] * planes[b, c]
            psi[(step * (flat // LANES) + c) * deep:(step * (flat // LANES) + c) * deep + kk, :] = total
    for step in range(n_band):
        for c in range(flat // LANES):
            top = (step * (flat // LANES) + c) * deep
            ppart_ref[step, c * part:(c + 1) * part, :] = psi[pl.ds(top + half * part, part), :]
    for copy in copies[2:]:
        copy.wait()
    tile = tile_ref[0:1, :]
    feat_ref[0] = ((tile // n_tx) * side + offset_ref[0:1, :]).astype(F32)
    feat_ref[1] = ((tile % n_tx) * side + offset_ref[1:2, :]).astype(F32)
    feat_ref[2] = scale_ref[0:1, :].astype(F32)
    for t in range(taylor):
        feat_ref[3 + t] = amp_ref[t:t + 1, :]
    for step in range(n_band):
        to = me ^ step
        total = w_ref[0, to] * dirty_ref[0]
        for b in range(1, bands):
            total = total + w_ref[b, to] * dirty_ref[b]
        dpart_ref[step] = total


def prep(dirty, psf, comp_tile, comp_offset, comp_scale, comp_amp, fit_weight, me, half, n_tx, n_band):
    bands, kk, flat = psf.shape
    listed, taylor = comp_amp.shape
    feats, deep = 3 + taylor, -(-kk // 8) * 8
    rows = (kk // 2) * (flat // LANES)
    args = (fit_weight, comp_tile.T, comp_offset.T, comp_scale[None], comp_amp.T, dirty, psf.transpose(1, 0, 2))
    return pl.pallas_call(
        functools.partial(prep_kernel, me=me, half=half, n_tx=n_tx, n_band=n_band),
        out_shape=(
            jax.ShapeDtypeStruct((feats, 1, listed), F32),
            jax.ShapeDtypeStruct((n_band,) + dirty.shape[1:], F32),
            jax.ShapeDtypeStruct((n_band, rows, LANES), F32),
            jax.ShapeDtypeStruct(psf.shape, F32),
        ),
        in_specs=[pl.BlockSpec(memory_space=pltpu.HBM)] * len(args),
        out_specs=(vmem(),) * 4,
        scratch_shapes=[pltpu.SMEM(args[0].shape, F32)] + [pltpu.VMEM(x.shape, x.dtype) for x in args[1:]] + [
            pltpu.VMEM((bands * kk * (flat // LANES), LANES), F32),
            pltpu.VMEM((n_band * deep * (flat // LANES), LANES), F32),
            pltpu.SemaphoreType.DMA((len(args),))],
        compiler_params=pltpu.CompilerParams(vmem_limit_bytes=12 * 1024 * 1024),
    )(*[pltpu.with_memory_space_constraint(x, pltpu.HBM) for x in args])


def pick(chunk, first, dest, lane, patch):
    c, off = divmod(first, LANES)
    a = chunk(c)
    if off + patch > LANES:
        a = jnp.where(lane >= off, a, chunk(c + 1))
    turn = (dest - off) % LANES
    return pltpu.roll(a, turn, 1) if turn else a


def pack_kernel(psf_ref, out_ref, *, patch):
    kk = psf_ref.shape[1]
    planes = [psf_ref[b] for b in range(2)]
    lane = lax.broadcasted_iota(I32, (kk, LANES), 1)
    for u in range(patch):
        two = [pick(lambda c, x=x: x[:, c * LANES:(c + 1) * LANES], u * patch, b * HALF, lane, patch)
               for b, x in enumerate(planes)]
        v = jnp.where(lane < HALF, two[0], two[1])
        out_ref[pl.ds(u, kk, stride=patch), :] = jnp.where(lane % HALF < patch, v, 0.0)


def pack(psf, patch):
    return pl.pallas_call(
        functools.partial(pack_kernel, patch=patch),
        out_shape=jax.ShapeDtypeStruct((psf.shape[1] * patch, LANES), F32),
        in_specs=[vmem()], out_specs=vmem(),
        compiler_params=pltpu.CompilerParams(vmem_limit_bytes=4 * 1024 * 1024),
    )(psf)


def pack_fit_kernel(mine_ref, other_ref, out_ref, *, patch, half):
    h = patch // 2
    n = mine_ref.shape[0] // (patch * patch // LANES)
    half = half()
    lane = lax.broadcasted_iota(I32, (n, LANES), 1)
    for ref, start in ((mine_ref, half), (other_ref, 1 - half)):
        chunk = lambda c: ref[c * n:(c + 1) * n, :]
        for u in range(h):
            v = jnp.where(lane < HALF, pick(chunk, u * patch, 0, lane, patch),
                          pick(chunk, (u + h) * patch, HALF, lane, patch))
            out_ref[pl.ds(start * (n * h) + u, n, stride=h), :] = jnp.where(lane % HALF < patch, v, 0.0)


def pack_fit(mine, other, patch, half):
    n = mine.shape[0] // (patch * patch // LANES)
    return pl.pallas_call(
        functools.partial(pack_fit_kernel, patch=patch, half=half),
        out_shape=jax.ShapeDtypeStruct((2 * n * (patch // 2), LANES), F32),
        in_specs=[vmem()] * 2, out_specs=vmem(),
        compiler_params=pltpu.CompilerParams(vmem_limit_bytes=4 * 1024 * 1024),
    )(mine, other)


def render_kernel(feat_ref, g_ref, gt_ref, dirty_ref, res_ref, tay_ref,
                  words_v, list_v, words_s, amps_s, list_s, acc, acct, sems, *,
                  patch, tile, taylor, scales, origin):
    rows = tile + 2 * patch
    S = feat_ref.shape[1]
    h = patch // 2
    c1 = pltpu.make_async_copy(feat_ref.at[pl.ds(3, taylor)], amps_s.at[:, pl.ds(0, S), :], sems.at[0])
    c1.start()
    r0, c0 = origin()
    rr = feat_ref[0].astype(I32) - r0
    cc = feat_ref[1].astype(I32) - c0
    mask = (rr > -patch) & (rr < tile) & (cc > -patch) & (cc < tile)
    base = jnp.where(mask, ((cc + HALF) >> 6) * rows + rr + patch, 0)
    words_v[...] = base + ((cc & (LANES - 1)) << 14) + (feat_ref[2].astype(I32) << 21)
    c2 = pltpu.make_async_copy(words_v, words_s.at[pl.ds(0, S), :], sems.at[1])
    c2.start()
    mb = jnp.where(mask, 1.0, 0.0).astype(BF16)
    i0 = lax.broadcasted_iota(I32, (LANES, LANES), 0)
    i1 = lax.broadcasted_iota(I32, (LANES, LANES), 1)
    upper = jnp.where(i0 < i1, 1.0, 0.0).astype(BF16)
    ones = jnp.ones((LANES, LANES), BF16)
    s0 = lax.broadcasted_iota(I32, (S, S), 0)
    s1 = lax.broadcasted_iota(I32, (S, S), 1)
    below = jnp.where(s1 < s0, 1.0, 0.0).astype(BF16)
    before = jnp.dot(below, mb, preferred_element_type=F32).astype(BF16)
    every = jnp.dot(jnp.ones((8, S), BF16), mb, preferred_element_type=F32).astype(BF16)
    rank = jnp.dot(mb, upper, preferred_element_type=F32) + jnp.dot(before, ones, preferred_element_type=F32)
    total = jnp.dot(every, ones, preferred_element_type=F32)
    list_v[S:S + 8, :] = total.astype(I32)
    rank = jnp.where(mask, rank, -1.0).astype(I32)
    lo, hi = rank & (LANES - 1), rank >> 7
    lane_row = lax.broadcasted_iota(I32, (S, LANES), 1).astype(F32)
    srow = lax.broadcasted_iota(I32, (S, LANES), 0)
    got = None
    for d in range(S):
        hit = hi[d:d + 1, :] == srow
        onehot = jnp.where(lo[d:d + 1, :] == i0, 1.0, 0.0).astype(BF16)
        pair = [jnp.where(hit, lane_row, 0.0), jnp.where(hit, float(d), 0.0)]
        one = lax.dot_general(jnp.concatenate(pair, 0).astype(BF16), onehot, (((1,), (1,)), ((), ())),
                              preferred_element_type=F32)
        got = one if got is None else got + one
    list_v[0:S, :] = got[S:].astype(I32) * LANES + got[:S].astype(I32)
    c3 = pltpu.make_async_copy(list_v, list_s, sems.at[2])
    c3.start()
    for j in range(1, acc.shape[0] // rows - 1):
        acc[pl.ds(j * rows + patch, tile), :] = jnp.zeros((tile, LANES), F32)
        acct[pl.ds(j * rows + patch - h, tile + h), :] = jnp.zeros((tile + h, LANES), F32)
    c1.wait()
    c2.wait()
    c3.wait()
    for t in range(taylor):
        amps_s[t, S, 0] = 0.0
    words_s[S, 0] = 0
    n = list_s[S, 0]
    lane_half = lax.broadcasted_iota(I32, (1, LANES), 1) & (HALF - 1)

    def gen(it, k):
        row, col = it // (LANES // U), (it % (LANES // U)) * U + k
        idx = jnp.where(it * U + k < n, list_s[row, col], S * LANES)
        row, col = idx >> 7, idx & (LANES - 1)
        word = words_s[row, col]
        base, turn, width = word & 16383, (word >> 14) & (LANES - 1), word >> 21
        gb, hb = pl.multiple_of(width * patch, 8), pl.multiple_of(width * h, 8)
        p = q = None
        for t in range(taylor):
            a = amps_s[t, row, col]
            x = a * g_ref[pl.ds(gb + t * scales * patch, patch), :]
            y = a * gt_ref[pl.ds(hb + t * scales * h, h), :]
            p, q = (x, y) if p is None else (p + x, q + y)
        p = p.astype(BF16).astype(F32)
        return pltpu.roll(p, turn, 1), pltpu.roll(q, turn, 1), base, turn & (HALF - 1)

    def put(p, q, base, turn):
        first = lane_half >= turn
        for ref, val, high in ((acc, p, patch), (acct, q, h)):
            here, right = pl.ds(base, high), pl.ds(base + rows, high)
            ref[here, :] = ref[here, :] + jnp.where(first, val, 0.0)
            ref[right, :] = ref[right, :] + jnp.where(first, 0.0, val)

    def step(i, carry):
        for item in [gen(i, k) for k in range(U)]:
            put(*item)
        return carry

    lax.fori_loop(0, (n + U - 1) // U, step, 0)

    left = lax.broadcasted_iota(I32, (tile, LANES), 1) < HALF
    for c in range(tile // LANES):
        j, cols = 2 * c + 1, slice(c * LANES, (c + 1) * LANES)

        def get(ref, jj, top):
            return ref[pl.ds(jj * rows + top, tile), :]

        x, y = get(acc, j, patch), get(acc, j + 1, patch)
        res_ref[0, :, cols] = dirty_ref[0, :, cols] - jnp.where(left, x, y)
        res_ref[1, :, cols] = dirty_ref[1, :, cols] - pltpu.roll(jnp.where(left, y, x), HALF, 1)
        up = jnp.where(left, get(acct, j, patch), get(acct, j + 1, patch))
        low = pltpu.roll(jnp.where(left, get(acct, j + 1, patch - h), get(acct, j, patch - h)), HALF, 1)
        tay_ref[0, :, cols] = up + low


def render(feats, g, gt, dirty, origin, *, patch, taylor, scales):
    tile, S = dirty.shape[1], feats.shape[1]
    rows, tiles = tile + 2 * patch, tile // HALF + 2
    return pl.pallas_call(
        functools.partial(render_kernel, patch=patch, tile=tile, taylor=taylor, scales=scales, origin=origin),
        out_shape=(jax.ShapeDtypeStruct(dirty.shape, F32), jax.ShapeDtypeStruct((1,) + dirty.shape[1:], F32)),
        in_specs=[vmem()] * 4, out_specs=(vmem(),) * 2,
        scratch_shapes=[
            pltpu.VMEM((S, LANES), I32), pltpu.VMEM((S + 8, LANES), I32),
            pltpu.SMEM((S + 1, LANES), I32), pltpu.SMEM((taylor, S + 1, LANES), F32), pltpu.SMEM((S + 8, LANES), I32),
            pltpu.VMEM((tiles * rows, LANES), F32), pltpu.VMEM((tiles * rows, LANES), F32),
            pltpu.SemaphoreType.DMA((3,))],
        compiler_params=pltpu.CompilerParams(vmem_limit_bytes=8 * 1024 * 1024),
    )(feats, g, gt, dirty)


def per_device(dirty, psf, comp_tile, comp_offset, comp_scale, comp_amp, fit_weight):
    bands, tile = dirty.shape[0], dirty.shape[1]
    patch = math.isqrt(psf.shape[2])
    taylor = comp_amp.shape[1]
    scales = psf.shape[1] // taylor
    n_ty, n_tx, n_band = lax.axis_size("ty"), lax.axis_size("tx"), lax.axis_size("band")
    half = lambda: lax.axis_index("ty") % 2
    feats, dirty_parts, psi_parts, planes = prep(
        dirty, psf, comp_tile, comp_offset, comp_scale, comp_amp, fit_weight,
        lambda: lax.axis_index("band"), half, n_tx, n_band)
    lift = 2.0 ** math.floor(math.log2(60000.0 / (bands * 30.0)))

    def sent(parts):
        return [lax.ppermute((parts[s] * lift).astype(jnp.float16), "band", [(i, i ^ s) for i in range(n_band)])
                for s in range(1, n_band)]

    def summed(parts, got):
        total = parts[0]
        for value in got:
            total = total + value.astype(F32) * (1.0 / lift)
        return total

    psi = summed(psi_parts, sent(psi_parts))
    dirty_got = sent(dirty_parts)
    bit = 1
    while bit < n_ty * n_tx:
        other = lax.ppermute(feats, ("ty", "tx"), [(i, i ^ bit) for i in range(n_ty * n_tx)])
        feats = jnp.concatenate([feats, other], 1)
        bit *= 2
    psi_other = lax.ppermute(psi, "ty", [(i, i ^ 1) for i in range(n_ty)])
    residual, model_fit = render(
        feats, pack(planes, patch), pack_fit(psi, psi_other, patch, half), dirty,
        lambda: (lax.axis_index("ty") * tile, lax.axis_index("tx") * tile),
        patch=patch, taylor=taylor, scales=scales)
    return residual, summed(dirty_parts, dirty_got)[None] - model_fit


def solution(mesh):
    return jax.shard_map(
        per_device,
        mesh=mesh,
        in_specs=(
            P("band", "ty", "tx"),
            P("band", None, None),
            P(("ty", "tx"), None),
            P(("ty", "tx"), None),
            P(("ty", "tx")),
            P(("ty", "tx"), None),
            P("band", None),
        ),
        out_specs=(P("band", "ty", "tx"), P("band", "ty", "tx")),
        check_vma=False,
    )
```

```python
import functools
import math
import jax
import jax.numpy as jnp
from jax import lax
from jax.experimental import pallas as pl
from jax.experimental.pallas import tpu as pltpu
from jax.sharding import PartitionSpec as P

LANES = 128
HALF = 64
U = 16
LIST = 8
F32, BF16, I32 = jnp.float32, jnp.bfloat16, jnp.int32


def vmem():
    return pl.BlockSpec(memory_space=pltpu.VMEM)


def prep_kernel(w_hbm, tile_hbm, offset_hbm, scale_hbm, amp_hbm, dirty_hbm, psf_hbm,
                feat_ref, pay_ref, keep_ref, dsend_ref, dkeep_ref, plane_ref,
                w_ref, tile_ref, offset_ref, scale_ref, amp_ref, dirty_ref, psf_ref, pairs, psi, sems, *,
                me, share, shares, n_tx, n_band, lift):
    copies = [pltpu.make_async_copy(src, dst, sems.at[i]) for i, (src, dst) in enumerate((
        (psf_hbm, psf_ref), (w_hbm, w_ref), (tile_hbm, tile_ref), (offset_hbm, offset_ref),
        (scale_hbm, scale_ref), (amp_hbm, amp_ref), (dirty_hbm, dirty_ref)))]
    for copy in copies:
        copy.start()
    bands, side = dirty_ref.shape[0], dirty_ref.shape[1]
    kk, flat = psf_ref.shape[0], psf_ref.shape[2]
    chunks = flat // LANES
    taylor = amp_ref.shape[0]
    me, share = me(), share()
    part, deep, block = kk // shares, -(-kk // 8) * 8, keep_ref.shape[1]
    copies[0].wait()
    copies[1].wait()
    for c in range(chunks):
        for k in range(kk):
            top = (c * kk + k) * bands
            pairs[top:top + bands, :] = psf_ref[k, :, c * LANES:(c + 1) * LANES].astype(F32)
    planes = {}
    for c in range(chunks):
        for b in range(bands):
            planes[b, c] = pairs[pl.ds(c * bands * kk + b, kk, stride=bands), :]
            plane_ref[b, :, c * LANES:(c + 1) * LANES] = planes[b, c]
    for step in range(n_band):
        for c in range(chunks):
            total = w_ref[0, me ^ step] * planes[0, c]
            for b in range(1, bands):
                total = total + w_ref[b, me ^ step] * planes[b, c]
            psi[(step * chunks + c) * deep:(step * chunks + c) * deep + kk, :] = total
    spare = jnp.zeros((block - part * chunks, LANES), F32)
    for step in range(n_band):
        for c in range(chunks):
            rows = psi[pl.ds((step * chunks + c) * deep + share * part, part), :]
            if step % 2:
                pay_ref[step // 2, c * part:(c + 1) * part, :] = rows * lift
            else:
                keep_ref[step // 2, c * part:(c + 1) * part, :] = rows
        (pay_ref if step % 2 else keep_ref)[step // 2, part * chunks:, :] = spare
    for copy in copies[2:]:
        copy.wait()
    tile = tile_ref[0:1, :]
    feat_ref[0:1, :] = ((tile // n_tx) * side + offset_ref[0:1, :]).astype(F32)
    feat_ref[1:2, :] = ((tile % n_tx) * side + offset_ref[1:2, :]).astype(F32)
    feat_ref[2:3, :] = scale_ref[0:1, :].astype(F32)
    feat_ref[3:3 + taylor, :] = amp_ref[...]
    feat_ref[3 + taylor:, :] = jnp.zeros((LIST - 3 - taylor, LANES), F32)
    for step in range(n_band):
        total = w_ref[0, me ^ step] * dirty_ref[0]
        for b in range(1, bands):
            total = total + w_ref[b, me ^ step] * dirty_ref[b]
        if step % 2:
            dsend_ref[step // 2] = total * lift
        else:
            dkeep_ref[step // 2] = total


def prep(dirty, psf, comp_tile, comp_offset, comp_scale, comp_amp, fit_weight, me, share, shares, n_tx, n_band, lift):
    bands, kk, flat = psf.shape
    side = dirty.shape[1]
    deep, chunks = -(-kk // 8) * 8, flat // LANES
    block = -(-(kk // shares) * chunks // 16) * 16
    args = (fit_weight, comp_tile.T, comp_offset.T, comp_scale[None], comp_amp.T, dirty, psf.transpose(1, 0, 2))
    return pl.pallas_call(
        functools.partial(prep_kernel, me=me, share=share, shares=shares, n_tx=n_tx, n_band=n_band, lift=lift),
        out_shape=(
            jax.ShapeDtypeStruct((LIST, LANES), F32),
            jax.ShapeDtypeStruct((n_band // 2, block, LANES), F32),
            jax.ShapeDtypeStruct((n_band // 2, block, LANES), F32),
            jax.ShapeDtypeStruct((n_band // 2, side, side), F32),
            jax.ShapeDtypeStruct((n_band // 2, side, side), F32),
            jax.ShapeDtypeStruct(psf.shape, F32),
        ),
        in_specs=[pl.BlockSpec(memory_space=pltpu.HBM)] * len(args),
        out_specs=(vmem(),) * 6,
        scratch_shapes=[pltpu.SMEM(args[0].shape, F32)] + [pltpu.VMEM(x.shape, x.dtype) for x in args[1:]] + [
            pltpu.VMEM((bands * kk * chunks, LANES), F32),
            pltpu.VMEM((n_band * deep * chunks, LANES), F32),
            pltpu.SemaphoreType.DMA((len(args),))],
        compiler_params=pltpu.CompilerParams(vmem_limit_bytes=12 * 1024 * 1024),
    )(*[pltpu.with_memory_space_constraint(x, pltpu.HBM) for x in args])


def pick(chunk, first, dest, lane, patch):
    c, off = divmod(first, LANES)
    a = chunk(c)
    if off + patch > LANES:
        a = jnp.where(lane >= off, a, chunk(c + 1))
    turn = (dest - off) % LANES
    return pltpu.roll(a, turn, 1) if turn else a


def pack_kernel(psf_ref, out_ref, *, patch):
    kk = psf_ref.shape[1]
    planes = [psf_ref[b] for b in range(2)]
    lane = lax.broadcasted_iota(I32, (kk, LANES), 1)
    for u in range(patch):
        two = [pick(lambda c, x=x: x[:, c * LANES:(c + 1) * LANES], u * patch, b * HALF, lane, patch)
               for b, x in enumerate(planes)]
        v = jnp.where(lane < HALF, two[0], two[1])
        out_ref[pl.ds(u, kk, stride=patch), :] = jnp.where(lane % HALF < patch, v, 0.0)


def pack(psf, patch):
    return pl.pallas_call(
        functools.partial(pack_kernel, patch=patch),
        out_shape=jax.ShapeDtypeStruct((psf.shape[1] * patch, LANES), F32),
        in_specs=[vmem()], out_specs=vmem(),
        compiler_params=pltpu.CompilerParams(vmem_limit_bytes=4 * 1024 * 1024),
    )(psf)


def pack_fit_kernel(psi_ref, out_ref, *, patch, shares, start):
    h = patch // 2
    n, block = out_ref.shape[0] // h // shares, psi_ref.shape[0] // shares
    lane = lax.broadcasted_iota(I32, (n, LANES), 1)
    for s in range(shares):
        top = start(s) * (n * h)

        def chunk(c):
            return psi_ref[s * block + c * n:s * block + (c + 1) * n, :]

        for u in range(h):
            v = jnp.where(lane < HALF, pick(chunk, u * patch, 0, lane, patch),
                          pick(chunk, (u + h) * patch, HALF, lane, patch))
            out_ref[pl.ds(top + u, n, stride=h), :] = jnp.where(lane % HALF < patch, v, 0.0)


def pack_fit(psi, kk, patch, shares, start):
    return pl.pallas_call(
        functools.partial(pack_fit_kernel, patch=patch, shares=shares, start=start),
        out_shape=jax.ShapeDtypeStruct((kk * (patch // 2), LANES), F32),
        in_specs=[vmem()], out_specs=vmem(),
        compiler_params=pltpu.CompilerParams(vmem_limit_bytes=4 * 1024 * 1024),
    )(psi)


def render_kernel(list_ref, g_ref, gt_ref, dirty_ref, res_ref, tay_ref,
                  words_v, amps_v, list_v, words_s, amps_s, list_s, acc, acct, sems, *,
                  patch, tile, taylor, scales, origin):
    rows = tile + 2 * patch
    S = list_ref.shape[0] // LIST
    h = patch // 2

    def plane(n):
        return list_ref[pl.ds(n, S, stride=LIST), :]

    for t in range(taylor):
        amps_v[t] = plane(3 + t)
    c1 = pltpu.make_async_copy(amps_v, amps_s.at[:, pl.ds(0, S), :], sems.at[0])
    c1.start()
    r0, c0 = origin()
    rr = plane(0).astype(I32) - r0
    cc = plane(1).astype(I32) - c0
    mask = (rr > -patch) & (rr < tile) & (cc > -patch) & (cc < tile)
    base = jnp.where(mask, ((cc + HALF) >> 6) * rows + rr + patch, 0)
    words_v[...] = base + ((cc & (LANES - 1)) << 14) + (plane(2).astype(I32) << 21)
    c2 = pltpu.make_async_copy(words_v, words_s.at[pl.ds(0, S), :], sems.at[1])
    c2.start()
    mb = jnp.where(mask, 1.0, 0.0).astype(BF16)
    i0 = lax.broadcasted_iota(I32, (LANES, LANES), 0)
    i1 = lax.broadcasted_iota(I32, (LANES, LANES), 1)
    upper = jnp.where(i0 < i1, 1.0, 0.0).astype(BF16)
    ones = jnp.ones((LANES, LANES), BF16)
    s0 = lax.broadcasted_iota(I32, (S, S), 0)
    s1 = lax.broadcasted_iota(I32, (S, S), 1)
    below = jnp.where(s1 < s0, 1.0, 0.0).astype(BF16)
    before = jnp.dot(below, mb, preferred_element_type=F32).astype(BF16)
    every = jnp.dot(jnp.ones((8, S), BF16), mb, preferred_element_type=F32).astype(BF16)
    rank = jnp.dot(mb, upper, preferred_element_type=F32) + jnp.dot(before, ones, preferred_element_type=F32)
    total = jnp.dot(every, ones, preferred_element_type=F32)
    list_v[S:S + 8, :] = total.astype(I32)
    rank = jnp.where(mask, rank, -1.0).astype(I32)
    lo, hi = rank & (LANES - 1), rank >> 7
    lane_row = lax.broadcasted_iota(I32, (S, LANES), 1).astype(F32)
    srow = lax.broadcasted_iota(I32, (S, LANES), 0)
    got = None
    for d in range(S):
        hit = hi[d:d + 1, :] == srow
        onehot = jnp.where(lo[d:d + 1, :] == i0, 1.0, 0.0).astype(BF16)
        pair = [jnp.where(hit, lane_row, 0.0), jnp.where(hit, float(d), 0.0)]
        one = lax.dot_general(jnp.concatenate(pair, 0).astype(BF16), onehot, (((1,), (1,)), ((), ())),
                              preferred_element_type=F32)
        got = one if got is None else got + one
    list_v[0:S, :] = got[S:].astype(I32) * LANES + got[:S].astype(I32)
    c3 = pltpu.make_async_copy(list_v, list_s, sems.at[2])
    c3.start()
    for j in range(1, acc.shape[0] // rows - 1):
        acc[pl.ds(j * rows + patch, tile), :] = jnp.zeros((tile, LANES), F32)
        acct[pl.ds(j * rows + patch - h, tile + h), :] = jnp.zeros((tile + h, LANES), F32)
    c1.wait()
    c2.wait()
    c3.wait()
    for t in range(taylor):
        amps_s[t, S, 0] = 0.0
    words_s[S, 0] = 0
    n = list_s[S, 0]
    lane_half = lax.broadcasted_iota(I32, (1, LANES), 1) & (HALF - 1)

    def gen(it, k):
        row, col = it // (LANES // U), (it % (LANES // U)) * U + k
        idx = jnp.where(it * U + k < n, list_s[row, col], S * LANES)
        row, col = idx >> 7, idx & (LANES - 1)
        word = words_s[row, col]
        base, turn, width = word & 16383, (word >> 14) & (LANES - 1), word >> 21
        gb, hb = pl.multiple_of(width * patch, 8), pl.multiple_of(width * h, 8)
        p = q = None
        for t in range(taylor):
            a = amps_s[t, row, col]
            x = a * g_ref[pl.ds(gb + t * scales * patch, patch), :]
            y = a * gt_ref[pl.ds(hb + t * scales * h, h), :]
            p, q = (x, y) if p is None else (p + x, q + y)
        p = p.astype(BF16).astype(F32)
        return pltpu.roll(p, turn, 1), pltpu.roll(q, turn, 1), base, turn & (HALF - 1)

    def put(p, q, base, turn):
        first = lane_half >= turn
        for ref, val, high in ((acc, p, patch), (acct, q, h)):
            here, right = pl.ds(base, high), pl.ds(base + rows, high)
            ref[here, :] = ref[here, :] + jnp.where(first, val, 0.0)
            ref[right, :] = ref[right, :] + jnp.where(first, 0.0, val)

    def step(i, carry):
        for item in [gen(i, k) for k in range(U)]:
            put(*item)
        return carry

    lax.fori_loop(0, (n + U - 1) // U, step, 0)

    left = lax.broadcasted_iota(I32, (tile, LANES), 1) < HALF
    for c in range(tile // LANES):
        j, cols = 2 * c + 1, slice(c * LANES, (c + 1) * LANES)

        def get(ref, jj, top):
            return ref[pl.ds(jj * rows + top, tile), :]

        x, y = get(acc, j, patch), get(acc, j + 1, patch)
        res_ref[0, :, cols] = dirty_ref[0, :, cols] - jnp.where(left, x, y)
        res_ref[1, :, cols] = dirty_ref[1, :, cols] - pltpu.roll(jnp.where(left, y, x), HALF, 1)
        up = jnp.where(left, get(acct, j, patch), get(acct, j + 1, patch))
        low = pltpu.roll(jnp.where(left, get(acct, j + 1, patch - h), get(acct, j, patch - h)), HALF, 1)
        tay_ref[0, :, cols] = up + low


def render(lists, g, gt, dirty, origin, *, patch, taylor, scales):
    tile, S = dirty.shape[1], lists.shape[0] // LIST
    rows, tiles = tile + 2 * patch, tile // HALF + 2
    return pl.pallas_call(
        functools.partial(render_kernel, patch=patch, tile=tile, taylor=taylor, scales=scales, origin=origin),
        out_shape=(jax.ShapeDtypeStruct(dirty.shape, F32), jax.ShapeDtypeStruct((1,) + dirty.shape[1:], F32)),
        in_specs=[vmem()] * 4, out_specs=(vmem(),) * 2,
        scratch_shapes=[
            pltpu.VMEM((S, LANES), I32), pltpu.VMEM((taylor, S, LANES), F32), pltpu.VMEM((S + 8, LANES), I32),
            pltpu.SMEM((S + 1, LANES), I32), pltpu.SMEM((taylor, S + 1, LANES), F32), pltpu.SMEM((S + 8, LANES), I32),
            pltpu.VMEM((tiles * rows, LANES), F32), pltpu.VMEM((tiles * rows, LANES), F32),
            pltpu.SemaphoreType.DMA((3,))],
        compiler_params=pltpu.CompilerParams(vmem_limit_bytes=8 * 1024 * 1024),
    )(lists, g, gt, dirty)


def per_device(dirty, psf, comp_tile, comp_offset, comp_scale, comp_amp, fit_weight):
    bands, tile = dirty.shape[0], dirty.shape[1]
    patch = math.isqrt(psf.shape[2])
    taylor = comp_amp.shape[1]
    scales = psf.shape[1] // taylor
    n_ty, n_tx, n_band = lax.axis_size("ty"), lax.axis_size("tx"), lax.axis_size("band")
    lift = 2.0 ** math.floor(math.log2(65504.0 / (bands * 30.0)))
    bits = [1 << n for n in range((n_tx - 1).bit_length())]
    bits += [n_tx << n for n in range(1, (n_ty - 1).bit_length())] + [n_tx]
    shares = 2

    def share():
        return lax.axis_index("ty") % 2

    lists, psi_send, psi_keep, dirty_send, dirty_keep, planes = prep(
        dirty, psf, comp_tile, comp_offset, comp_scale, comp_amp, fit_weight,
        lambda: lax.axis_index("band"), share, shares, n_tx, n_band, lift)

    def across(value, bit):
        got = lax.ppermute(value.astype(jnp.float16), "band", [(i, i ^ bit) for i in range(n_band)])
        return got.astype(F32) * (1.0 / lift)

    def hop(value, bit):
        return lax.ppermute(value, ("ty", "tx"), [(i, i ^ bit) for i in range(n_ty * n_tx)])

    psi = psi_keep + across(psi_send, 1)
    total = dirty_keep + across(dirty_send, 1)
    band_bits = [1 << n for n in range(1, (n_band - 1).bit_length())]
    for n, bit in enumerate(band_bits):
        cut = psi.shape[0] // 2
        got = across(psi[cut:] * lift, bit)
        psi = psi[:cut] + got
    for bit in bits[:-1]:
        lists = jnp.concatenate([lists, hop(lists, bit)], 0)
    cut = lists.shape[0]
    out = jnp.concatenate([lists, psi[0]], 0)
    got = hop(out, bits[-1])
    lists = jnp.concatenate([lists, got[:cut]], 0)
    psi = jnp.concatenate([psi[0], got[cut:]], 0)
    for bit in band_bits:
        cut = total.shape[0] // 2
        total = total[:cut] + across(total[cut:] * lift, bit)
    residual, model_fit = render(
        lists, pack(planes, patch), pack_fit(psi, psf.shape[1], patch, shares, lambda s: share() ^ s), dirty,
        lambda: (lax.axis_index("ty") * tile, lax.axis_index("tx") * tile),
        patch=patch, taylor=taylor, scales=scales)
    return residual, total - model_fit


def solution(mesh):
    return jax.shard_map(
        per_device,
        mesh=mesh,
        in_specs=(
            P("band", "ty", "tx"),
            P("band", None, None),
            P(("ty", "tx"), None),
            P(("ty", "tx"), None),
            P(("ty", "tx")),
            P(("ty", "tx"), None),
            P("band", None),
        ),
        out_specs=(P("band", "ty", "tx"), P("band", "ty", "tx")),
        check_vma=False,
    )
```

```python
import functools
import math
import jax
import jax.numpy as jnp
from jax import lax
from jax.experimental import pallas as pl
from jax.experimental.pallas import tpu as pltpu
from jax.sharding import PartitionSpec as P

LANES = 128
HALF = 64
U = 16
LIST = 8
F32, BF16, I32 = jnp.float32, jnp.bfloat16, jnp.int32


def vmem():
    return pl.BlockSpec(memory_space=pltpu.VMEM)


def prep_kernel(w_hbm, tile_hbm, offset_hbm, scale_hbm, amp_hbm, dirty_hbm, psf_hbm,
                feat_ref, pay_ref, keep_ref, dsend_ref, dkeep_ref, pairs,
                w_ref, tile_ref, offset_ref, scale_ref, amp_ref, dirty_ref, psf_ref, sems, *,
                me, share, shares, n_tx, n_band, lift):
    copies = [pltpu.make_async_copy(src, dst, sems.at[i]) for i, (src, dst) in enumerate((
        (psf_hbm, psf_ref), (w_hbm, w_ref), (tile_hbm, tile_ref), (offset_hbm, offset_ref),
        (scale_hbm, scale_ref), (amp_hbm, amp_ref), (dirty_hbm, dirty_ref)))]
    for copy in copies:
        copy.start()
    bands, side = dirty_ref.shape[0], dirty_ref.shape[1]
    kk, flat = psf_ref.shape[0], psf_ref.shape[2]
    chunks = flat // LANES
    taylor = amp_ref.shape[0]
    me, share = me(), share()
    part, block = kk // shares, keep_ref.shape[1]
    copies[0].wait()
    copies[1].wait()
    for c in range(chunks):
        for k in range(kk):
            top = (c * kk + k) * bands
            pairs[top:top + bands, :] = psf_ref[k, :, c * LANES:(c + 1) * LANES].astype(F32)
    weights = [[w_ref[b, me ^ step] * (lift if step % 2 else 1.0) for b in range(bands)] for step in range(n_band)]
    for c in range(chunks):
        rows = [pairs[pl.ds((c * kk + share * part) * bands + b, part, stride=bands), :] for b in range(bands)]
        for step in range(n_band):
            total = weights[step][0] * rows[0]
            for b in range(1, bands):
                total = total + weights[step][b] * rows[b]
            (pay_ref if step % 2 else keep_ref)[step // 2, c * part:(c + 1) * part, :] = total
    spare = jnp.zeros((block - part * chunks, LANES), F32)
    for step in range(n_band):
        (pay_ref if step % 2 else keep_ref)[step // 2, part * chunks:, :] = spare
    for copy in copies[2:]:
        copy.wait()
    tile = tile_ref[0:1, :]
    feat_ref[0:1, :] = ((tile // n_tx) * side + offset_ref[0:1, :]).astype(F32)
    feat_ref[1:2, :] = ((tile % n_tx) * side + offset_ref[1:2, :]).astype(F32)
    feat_ref[2:3, :] = scale_ref[0:1, :].astype(F32)
    feat_ref[3:3 + taylor, :] = amp_ref[...]
    feat_ref[3 + taylor:, :] = jnp.zeros((LIST - 3 - taylor, LANES), F32)
    for step in range(n_band):
        total = weights[step][0] * dirty_ref[0]
        for b in range(1, bands):
            total = total + weights[step][b] * dirty_ref[b]
        (dsend_ref if step % 2 else dkeep_ref)[step // 2] = total


def prep(dirty, psf, comp_tile, comp_offset, comp_scale, comp_amp, fit_weight, me, share, shares, n_tx, n_band, lift):
    bands, kk, flat = psf.shape
    side = dirty.shape[1]
    chunks = flat // LANES
    block = -(-(kk // shares) * chunks // 16) * 16
    args = (fit_weight, comp_tile.T, comp_offset.T, comp_scale[None], comp_amp.T, dirty, psf.transpose(1, 0, 2))
    return pl.pallas_call(
        functools.partial(prep_kernel, me=me, share=share, shares=shares, n_tx=n_tx, n_band=n_band, lift=lift),
        out_shape=(
            jax.ShapeDtypeStruct((LIST, LANES), F32),
            jax.ShapeDtypeStruct((n_band // 2, block, LANES), F32),
            jax.ShapeDtypeStruct((n_band // 2, block, LANES), F32),
            jax.ShapeDtypeStruct((n_band // 2, side, side), F32),
            jax.ShapeDtypeStruct((n_band // 2, side, side), F32),
            jax.ShapeDtypeStruct((bands * kk * chunks, LANES), F32),
        ),
        in_specs=[pl.BlockSpec(memory_space=pltpu.HBM)] * len(args),
        out_specs=(vmem(),) * 6,
        scratch_shapes=[pltpu.SMEM(args[0].shape, F32)] + [pltpu.VMEM(x.shape, x.dtype) for x in args[1:]] + [
            pltpu.SemaphoreType.DMA((len(args),))],
        compiler_params=pltpu.CompilerParams(vmem_limit_bytes=12 * 1024 * 1024),
    )(*[pltpu.with_memory_space_constraint(x, pltpu.HBM) for x in args])


def pick(chunk, first, dest, lane, patch):
    c, off = divmod(first, LANES)
    a = chunk(c)
    if off + patch > LANES:
        a = jnp.where(lane >= off, a, chunk(c + 1))
    turn = (dest - off) % LANES
    return pltpu.roll(a, turn, 1) if turn else a


def pack_kernel(pairs_ref, out_ref, *, patch):
    kk = out_ref.shape[0] // patch
    lane = lax.broadcasted_iota(I32, (kk, LANES), 1)

    def chunk(b, c):
        return pairs_ref[pl.ds(c * 2 * kk + b, kk, stride=2), :]

    for u in range(patch):
        two = [pick(functools.partial(chunk, b), u * patch, b * HALF, lane, patch) for b in range(2)]
        v = jnp.where(lane < HALF, two[0], two[1])
        out_ref[pl.ds(u, kk, stride=patch), :] = jnp.where(lane % HALF < patch, v, 0.0)


def pack(pairs, patch):
    return pl.pallas_call(
        functools.partial(pack_kernel, patch=patch),
        out_shape=jax.ShapeDtypeStruct((pairs.shape[0] // 2 // (patch * patch // LANES) * patch, LANES), F32),
        in_specs=[vmem()], out_specs=vmem(),
        compiler_params=pltpu.CompilerParams(vmem_limit_bytes=4 * 1024 * 1024),
    )(pairs)


def pack_fit_kernel(psi_ref, out_ref, *, patch, shares, start):
    h = patch // 2
    n, block = out_ref.shape[0] // h // shares, psi_ref.shape[0] // shares
    lane = lax.broadcasted_iota(I32, (n, LANES), 1)
    for s in range(shares):
        top = start(s) * (n * h)

        def chunk(c):
            return psi_ref[s * block + c * n:s * block + (c + 1) * n, :]

        for u in range(h):
            v = jnp.where(lane < HALF, pick(chunk, u * patch, 0, lane, patch),
                          pick(chunk, (u + h) * patch, HALF, lane, patch))
            out_ref[pl.ds(top + u, n, stride=h), :] = jnp.where(lane % HALF < patch, v, 0.0)


def pack_fit(psi, kk, patch, shares, start):
    return pl.pallas_call(
        functools.partial(pack_fit_kernel, patch=patch, shares=shares, start=start),
        out_shape=jax.ShapeDtypeStruct((kk * (patch // 2), LANES), F32),
        in_specs=[vmem()], out_specs=vmem(),
        compiler_params=pltpu.CompilerParams(vmem_limit_bytes=4 * 1024 * 1024),
    )(psi)


def list_kernel(list_ref, words_ref, amps_ref, piece_v, rank_v, *, patch, tile, taylor, origin):
    rows = tile + 2 * patch
    S = list_ref.shape[0] // LIST

    def plane(n):
        return list_ref[pl.ds(n, S, stride=LIST), :]

    r0, c0 = origin()
    rr = plane(0).astype(I32) - r0
    cc = plane(1).astype(I32) - c0
    mask = (rr > -patch) & (rr < tile) & (cc > -patch) & (cc < tile)
    mb = jnp.where(mask, 1.0, 0.0).astype(BF16)
    i0 = lax.broadcasted_iota(I32, (LANES, LANES), 0)
    i1 = lax.broadcasted_iota(I32, (LANES, LANES), 1)
    upper = jnp.where(i0 < i1, 1.0, 0.0).astype(BF16)
    ones = jnp.ones((LANES, LANES), BF16)
    s0 = lax.broadcasted_iota(I32, (S, S), 0)
    s1 = lax.broadcasted_iota(I32, (S, S), 1)
    below = jnp.where(s1 < s0, 1.0, 0.0).astype(BF16)
    before = jnp.dot(below, mb, preferred_element_type=F32).astype(BF16)
    every = jnp.dot(jnp.ones((8, S), BF16), mb, preferred_element_type=F32).astype(BF16)
    rank = jnp.dot(mb, upper, preferred_element_type=F32) + jnp.dot(before, ones, preferred_element_type=F32)
    words_ref[S:S + 8, :] = jnp.dot(every, ones, preferred_element_type=F32).astype(I32)
    rank_v[...] = jnp.where(mask, rank, -1.0).astype(I32)
    base = jnp.where(mask, ((cc + HALF) >> 6) * rows + rr + patch, 0)
    word = base + ((cc & (LANES - 1)) << 14) + (plane(2).astype(I32) << 21)
    pieces = [(word & 255).astype(F32), ((word >> 8) & 255).astype(F32), ((word >> 16) & 255).astype(F32)]
    for t in range(taylor):
        rest = plane(3 + t)
        for _ in range(3):
            pieces.append(rest.astype(BF16).astype(F32))
            rest = rest - pieces[-1]
    for n, piece in enumerate(pieces):
        piece_v[n * S:(n + 1) * S, :] = piece
    srow = lax.broadcasted_iota(I32, (S, LANES), 0)

    def spread(d, got):
        rank = rank_v[pl.ds(d, 1), :]
        hit = (rank >> 7) == srow
        onehot = jnp.where((rank & (LANES - 1)) == i0, 1.0, 0.0).astype(BF16)
        lhs = jnp.concatenate([jnp.where(hit, piece_v[pl.ds(n * S + d, 1), :], 0.0) for n in range(len(pieces))], 0)
        return got + lax.dot_general(lhs.astype(BF16), onehot, (((1,), (1,)), ((), ())), preferred_element_type=F32)

    got = jnp.zeros((len(pieces) * S, LANES), F32)
    if S <= 16:
        for d in range(S):
            got = spread(d, got)
    else:
        got = lax.fori_loop(0, S, spread, got)
    part = [got[n * S:(n + 1) * S] for n in range(len(pieces))]
    words_ref[0:S, :] = part[0].astype(I32) + (part[1].astype(I32) << 8) + (part[2].astype(I32) << 16)
    for t in range(taylor):
        amps_ref[t * S:(t + 1) * S, :] = part[3 + 3 * t] + (part[4 + 3 * t] + part[5 + 3 * t])


def overlapping(lists, origin, *, patch, tile, taylor):
    S = lists.shape[0] // LIST
    return pl.pallas_call(
        functools.partial(list_kernel, patch=patch, tile=tile, taylor=taylor, origin=origin),
        out_shape=(jax.ShapeDtypeStruct((S + 8, LANES), I32), jax.ShapeDtypeStruct((taylor * S, LANES), F32)),
        in_specs=[vmem()], out_specs=(vmem(),) * 2,
        scratch_shapes=[pltpu.VMEM(((3 + 3 * taylor) * S, LANES), F32), pltpu.VMEM((S, LANES), I32)],
        compiler_params=pltpu.CompilerParams(vmem_limit_bytes=8 * 1024 * 1024),
    )(lists)


def render_kernel(words_ref, amps_ref, g_ref, gt_ref, dirty_hbm, res_ref, tay_ref,
                  words_s, amps_s, dirty_ref, acc, acct, sems, *, patch, tile, taylor, scales):
    rows = tile + 2 * patch
    S = words_ref.shape[0] - 8
    h = patch // 2
    copies = (pltpu.make_async_copy(words_ref, words_s, sems.at[0]),
              pltpu.make_async_copy(amps_ref, amps_s, sems.at[1]),
              pltpu.make_async_copy(dirty_hbm, dirty_ref, sems.at[2]))
    for copy in copies:
        copy.start()
    for j in range(1, acc.shape[0] // rows - 1):
        acc[pl.ds(j * rows + patch, tile), :] = jnp.zeros((tile, LANES), F32)
        acct[pl.ds(j * rows + patch - h, tile + h), :] = jnp.zeros((tile + h, LANES), F32)
    for copy in copies[:2]:
        copy.wait()
    n = words_s[S, 0]
    lane_half = lax.broadcasted_iota(I32, (1, LANES), 1) & (HALF - 1)

    def gen(it, k):
        row, col = it // (LANES // U), (it % (LANES // U)) * U + k
        word = words_s[row, col]
        base, turn, width = word & 16383, (word >> 14) & (LANES - 1), word >> 21
        gb, hb = pl.multiple_of(width * patch, 8), pl.multiple_of(width * h, 8)
        p = q = None
        for t in range(taylor):
            a = amps_s[row + t * S, col]
            x = a * g_ref[pl.ds(gb + t * scales * patch, patch), :]
            y = a * gt_ref[pl.ds(hb + t * scales * h, h), :]
            p, q = (x, y) if p is None else (p + x, q + y)
        p = p.astype(BF16).astype(F32)
        return pltpu.roll(p, turn, 1), pltpu.roll(q, turn, 1), base, turn & (HALF - 1)

    def put(p, q, base, turn):
        first = lane_half >= turn
        for ref, val, high in ((acc, p, patch), (acct, q, h)):
            here, right = pl.ds(base, high), pl.ds(base + rows, high)
            ref[here, :] = ref[here, :] + jnp.where(first, val, 0.0)
            ref[right, :] = ref[right, :] + jnp.where(first, 0.0, val)

    def step(i, carry):
        for item in [gen(i, k) for k in range(U)]:
            put(*item)
        return carry

    lax.fori_loop(0, (n + U - 1) // U, step, 0)

    copies[2].wait()
    left = lax.broadcasted_iota(I32, (tile, LANES), 1) < HALF
    for c in range(tile // LANES):
        j, cols = 2 * c + 1, slice(c * LANES, (c + 1) * LANES)

        def get(ref, jj, top):
            return ref[pl.ds(jj * rows + top, tile), :]

        x, y = get(acc, j, patch), get(acc, j + 1, patch)
        res_ref[0, :, cols] = dirty_ref[0, :, cols] - jnp.where(left, x, y)
        res_ref[1, :, cols] = dirty_ref[1, :, cols] - pltpu.roll(jnp.where(left, y, x), HALF, 1)
        up = jnp.where(left, get(acct, j, patch), get(acct, j + 1, patch))
        low = pltpu.roll(jnp.where(left, get(acct, j + 1, patch - h), get(acct, j, patch - h)), HALF, 1)
        tay_ref[0, :, cols] = up + low


def render(words, amps, g, gt, dirty, *, patch, taylor, scales):
    tile = dirty.shape[1]
    rows, tiles = tile + 2 * patch, tile // HALF + 2
    return pl.pallas_call(
        functools.partial(render_kernel, patch=patch, tile=tile, taylor=taylor, scales=scales),
        out_shape=(jax.ShapeDtypeStruct(dirty.shape, F32), jax.ShapeDtypeStruct((1,) + dirty.shape[1:], F32)),
        in_specs=[vmem()] * 4 + [pl.BlockSpec(memory_space=pltpu.HBM)], out_specs=(vmem(),) * 2,
        scratch_shapes=[
            pltpu.SMEM(words.shape, I32), pltpu.SMEM(amps.shape, F32), pltpu.VMEM(dirty.shape, F32),
            pltpu.VMEM((tiles * rows, LANES), F32), pltpu.VMEM((tiles * rows, LANES), F32),
            pltpu.SemaphoreType.DMA((3,))],
        compiler_params=pltpu.CompilerParams(vmem_limit_bytes=8 * 1024 * 1024),
    )(words, amps, g, gt, pltpu.with_memory_space_constraint(dirty, pltpu.HBM))


def per_device(dirty, psf, comp_tile, comp_offset, comp_scale, comp_amp, fit_weight):
    bands, tile = dirty.shape[0], dirty.shape[1]
    patch = math.isqrt(psf.shape[2])
    taylor = comp_amp.shape[1]
    scales = psf.shape[1] // taylor
    n_ty, n_tx, n_band = lax.axis_size("ty"), lax.axis_size("tx"), lax.axis_size("band")
    lift = 2.0 ** math.floor(math.log2(65504.0 / (bands * 30.0)))
    bits = [1 << n for n in range((n_tx - 1).bit_length())]
    bits += [n_tx << n for n in range(1, (n_ty - 1).bit_length())] + [n_tx]
    shares = 2

    def share():
        return lax.axis_index("ty") % 2

    lists, psi_send, psi_keep, dirty_send, dirty_keep, pairs = prep(
        dirty, psf, comp_tile, comp_offset, comp_scale, comp_amp, fit_weight,
        lambda: lax.axis_index("band"), share, shares, n_tx, n_band, lift)

    def across(value, bit):
        got = lax.ppermute(value.astype(jnp.float16), "band", [(i, i ^ bit) for i in range(n_band)])
        return got.astype(F32) * (1.0 / lift)

    def hop(value, bit):
        return lax.ppermute(value, ("ty", "tx"), [(i, i ^ bit) for i in range(n_ty * n_tx)])

    psi = psi_keep + across(psi_send, 1)
    total = dirty_keep + across(dirty_send, 1)
    band_bits = [1 << n for n in range(1, (n_band - 1).bit_length())]
    for n, bit in enumerate(band_bits):
        cut = psi.shape[0] // 2
        got = across(psi[cut:] * lift, bit)
        psi = psi[:cut] + got
    g = pack(pairs, patch)
    for bit in bits[:-1]:
        lists = jnp.concatenate([lists, hop(lists, bit)], 0)
    cut = lists.shape[0]
    got = hop(jnp.concatenate([lists, psi[0]], 0), bits[-1])
    lists = jnp.concatenate([lists, got[:cut]], 0)
    psi = jnp.concatenate([psi[0], got[cut:]], 0)
    words, amps = overlapping(
        lists, lambda: (lax.axis_index("ty") * tile, lax.axis_index("tx") * tile),
        patch=patch, tile=tile, taylor=taylor)
    for bit in band_bits:
        cut = total.shape[0] // 2
        total = total[:cut] + across(total[cut:] * lift, bit)
    residual, model_fit = render(
        words, amps, g, pack_fit(psi, psf.shape[1], patch, shares, lambda s: share() ^ s), dirty,
        patch=patch, taylor=taylor, scales=scales)
    return residual, total - model_fit


def solution(mesh):
    return jax.shard_map(
        per_device,
        mesh=mesh,
        in_specs=(
            P("band", "ty", "tx"),
            P("band", None, None),
            P(("ty", "tx"), None),
            P(("ty", "tx"), None),
            P(("ty", "tx")),
            P(("ty", "tx"), None),
            P("band", None),
        ),
        out_specs=(P("band", "ty", "tx"), P("band", "ty", "tx")),
        check_vma=False,
    )
```

```python
import functools
import math
import jax
import jax.numpy as jnp
from jax import lax
from jax.experimental import pallas as pl
from jax.experimental.pallas import tpu as pltpu
from jax.sharding import PartitionSpec as P

LANES = 128
HALF = 64
U = 16
LIST = 8
F32, BF16, I32 = jnp.float32, jnp.bfloat16, jnp.int32


def vmem():
    return pl.BlockSpec(memory_space=pltpu.VMEM)


def prep_kernel(w_hbm, tile_hbm, offset_hbm, scale_hbm, amp_hbm, dirty_hbm, psf_hbm,
                feat_ref, pay_ref, keep_ref, dsend_ref, dkeep_ref, pairs,
                w_ref, tile_ref, offset_ref, scale_ref, amp_ref, dirty_ref, psf_ref, sems, *,
                me, share, shares, n_tx, n_band, lift):
    copies = [pltpu.make_async_copy(src, dst, sems.at[i]) for i, (src, dst) in enumerate((
        (psf_hbm, psf_ref), (w_hbm, w_ref), (tile_hbm, tile_ref), (offset_hbm, offset_ref),
        (scale_hbm, scale_ref), (amp_hbm, amp_ref), (dirty_hbm, dirty_ref)))]
    for copy in copies:
        copy.start()
    bands, side = dirty_ref.shape[0], dirty_ref.shape[1]
    kk, flat = psf_ref.shape[0], psf_ref.shape[2]
    chunks = flat // LANES
    taylor = amp_ref.shape[0]
    me, share = me(), share()
    part, block = kk // shares, keep_ref.shape[1]
    copies[0].wait()
    copies[1].wait()
    for c in range(chunks):
        for k in range(kk):
            top = (c * kk + k) * bands
            pairs[top:top + bands, :] = psf_ref[k, :, c * LANES:(c + 1) * LANES].astype(F32)
    weights = [[w_ref[b, me ^ step] * (lift if step % 2 else 1.0) for b in range(bands)] for step in range(n_band)]
    for c in range(chunks):
        rows = [pairs[pl.ds((c * kk + share * part) * bands + b, part, stride=bands), :] for b in range(bands)]
        for step in range(n_band):
            total = weights[step][0] * rows[0]
            for b in range(1, bands):
                total = total + weights[step][b] * rows[b]
            (pay_ref if step % 2 else keep_ref)[step // 2, c * part:(c + 1) * part, :] = total
    spare = jnp.zeros((block - part * chunks, LANES), F32)
    for step in range(n_band):
        (pay_ref if step % 2 else keep_ref)[step // 2, part * chunks:, :] = spare
    for copy in copies[2:]:
        copy.wait()
    tile = tile_ref[0:1, :]
    feat_ref[0:1, :] = ((tile // n_tx) * side + offset_ref[0:1, :]).astype(F32)
    feat_ref[1:2, :] = ((tile % n_tx) * side + offset_ref[1:2, :]).astype(F32)
    feat_ref[2:3, :] = scale_ref[0:1, :].astype(F32)
    feat_ref[3:3 + taylor, :] = amp_ref[...]
    feat_ref[3 + taylor:, :] = jnp.zeros((LIST - 3 - taylor, LANES), F32)
    for step in range(n_band):
        total = weights[step][0] * dirty_ref[0]
        for b in range(1, bands):
            total = total + weights[step][b] * dirty_ref[b]
        (dsend_ref if step % 2 else dkeep_ref)[step // 2] = total


def prep(dirty, psf, comp_tile, comp_offset, comp_scale, comp_amp, fit_weight, me, share, shares, n_tx, n_band, lift):
    bands, kk, flat = psf.shape
    side = dirty.shape[1]
    chunks = flat // LANES
    block = -(-(kk // shares) * chunks // 16) * 16
    args = (fit_weight, comp_tile.T, comp_offset.T, comp_scale[None], comp_amp.T, dirty, psf.transpose(1, 0, 2))
    return pl.pallas_call(
        functools.partial(prep_kernel, me=me, share=share, shares=shares, n_tx=n_tx, n_band=n_band, lift=lift),
        out_shape=(
            jax.ShapeDtypeStruct((LIST, LANES), F32),
            jax.ShapeDtypeStruct((n_band // 2, block, LANES), F32),
            jax.ShapeDtypeStruct((n_band // 2, block, LANES), F32),
            jax.ShapeDtypeStruct((n_band // 2, side, side), F32),
            jax.ShapeDtypeStruct((n_band // 2, side, side), F32),
            jax.ShapeDtypeStruct((bands * kk * chunks, LANES), F32),
        ),
        in_specs=[pl.BlockSpec(memory_space=pltpu.HBM)] * len(args),
        out_specs=(vmem(),) * 6,
        scratch_shapes=[pltpu.SMEM(args[0].shape, F32)] + [pltpu.VMEM(x.shape, x.dtype) for x in args[1:]] + [
            pltpu.SemaphoreType.DMA((len(args),))],
        compiler_params=pltpu.CompilerParams(vmem_limit_bytes=12 * 1024 * 1024),
    )(*[pltpu.with_memory_space_constraint(x, pltpu.HBM) for x in args])


def pick(chunk, first, dest, lane, patch):
    c, off = divmod(first, LANES)
    a = chunk(c)
    if off + patch > LANES:
        a = jnp.where(lane >= off, a, chunk(c + 1))
    turn = (dest - off) % LANES
    return pltpu.roll(a, turn, 1) if turn else a


def pack_kernel(pairs_ref, out_ref, *, patch):
    kk = out_ref.shape[0] // patch
    lane = lax.broadcasted_iota(I32, (kk, LANES), 1)

    def chunk(b, c):
        return pairs_ref[pl.ds(c * 2 * kk + b, kk, stride=2), :]

    for u in range(patch):
        two = [pick(functools.partial(chunk, b), u * patch, b * HALF, lane, patch) for b in range(2)]
        v = jnp.where(lane < HALF, two[0], two[1])
        out_ref[pl.ds(u, kk, stride=patch), :] = jnp.where(lane % HALF < patch, v, 0.0)


def pack(pairs, patch):
    return pl.pallas_call(
        functools.partial(pack_kernel, patch=patch),
        out_shape=jax.ShapeDtypeStruct((pairs.shape[0] // 2 // (patch * patch // LANES) * patch, LANES), F32),
        in_specs=[vmem()], out_specs=vmem(),
        compiler_params=pltpu.CompilerParams(vmem_limit_bytes=4 * 1024 * 1024),
    )(pairs)


def pack_fit_kernel(psi_ref, out_ref, *, patch, shares, start):
    h = patch // 2
    n, block = out_ref.shape[0] // h // shares, psi_ref.shape[0] // shares
    lane = lax.broadcasted_iota(I32, (n, LANES), 1)
    for s in range(shares):
        top = start(s) * (n * h)

        def chunk(c):
            return psi_ref[s * block + c * n:s * block + (c + 1) * n, :]

        for u in range(h):
            v = jnp.where(lane < HALF, pick(chunk, u * patch, 0, lane, patch),
                          pick(chunk, (u + h) * patch, HALF, lane, patch))
            out_ref[pl.ds(top + u, n, stride=h), :] = jnp.where(lane % HALF < patch, v, 0.0)


def pack_fit(psi, kk, patch, shares, start):
    return pl.pallas_call(
        functools.partial(pack_fit_kernel, patch=patch, shares=shares, start=start),
        out_shape=jax.ShapeDtypeStruct((kk * (patch // 2), LANES), F32),
        in_specs=[vmem()], out_specs=vmem(),
        compiler_params=pltpu.CompilerParams(vmem_limit_bytes=4 * 1024 * 1024),
    )(psi)


def list_kernel(list_ref, words_ref, amps_ref, piece_v, rank_v, *, patch, tile, taylor, origin):
    rows = tile + 2 * patch
    S = list_ref.shape[0] // LIST

    def plane(n):
        return list_ref[pl.ds(n, S, stride=LIST), :]

    r0, c0 = origin()
    rr = plane(0).astype(I32) - r0
    cc = plane(1).astype(I32) - c0
    mask = (rr > -patch) & (rr < tile) & (cc > -patch) & (cc < tile)
    mb = jnp.where(mask, 1.0, 0.0).astype(BF16)
    i0 = lax.broadcasted_iota(I32, (LANES, LANES), 0)
    i1 = lax.broadcasted_iota(I32, (LANES, LANES), 1)
    upper = jnp.where(i0 < i1, 1.0, 0.0).astype(BF16)
    ones = jnp.ones((LANES, LANES), BF16)
    s0 = lax.broadcasted_iota(I32, (S, S), 0)
    s1 = lax.broadcasted_iota(I32, (S, S), 1)
    below = jnp.where(s1 < s0, 1.0, 0.0).astype(BF16)
    before = jnp.dot(below, mb, preferred_element_type=F32).astype(BF16)
    every = jnp.dot(jnp.ones((8, S), BF16), mb, preferred_element_type=F32).astype(BF16)
    rank = jnp.dot(mb, upper, preferred_element_type=F32) + jnp.dot(before, ones, preferred_element_type=F32)
    words_ref[S:S + 8, :] = jnp.dot(every, ones, preferred_element_type=F32).astype(I32)
    rank_v[...] = jnp.where(mask, rank, -1.0).astype(I32)
    base = jnp.where(mask, ((cc + HALF) >> 6) * rows + rr + patch, 0)
    word = base + ((cc & (LANES - 1)) << 14) + (plane(2).astype(I32) << 21)
    pieces = [(word & 255).astype(F32), ((word >> 8) & 255).astype(F32), ((word >> 16) & 255).astype(F32)]
    for t in range(taylor):
        rest = plane(3 + t)
        for _ in range(3):
            pieces.append(rest.astype(BF16).astype(F32))
            rest = rest - pieces[-1]
    for n, piece in enumerate(pieces):
        piece_v[n * S:(n + 1) * S, :] = piece
    srow = lax.broadcasted_iota(I32, (S, LANES), 0)

    def spread(d, got):
        rank = rank_v[pl.ds(d, 1), :]
        hit = (rank >> 7) == srow
        onehot = jnp.where((rank & (LANES - 1)) == i0, 1.0, 0.0).astype(BF16)
        lhs = jnp.concatenate([jnp.where(hit, piece_v[pl.ds(n * S + d, 1), :], 0.0) for n in range(len(pieces))], 0)
        return got + lax.dot_general(lhs.astype(BF16), onehot, (((1,), (1,)), ((), ())), preferred_element_type=F32)

    got = jnp.zeros((len(pieces) * S, LANES), F32)
    if S <= 16:
        for d in range(S):
            got = spread(d, got)
    else:
        got = lax.fori_loop(0, S, spread, got)
    part = [got[n * S:(n + 1) * S] for n in range(len(pieces))]
    words_ref[0:S, :] = part[0].astype(I32) + (part[1].astype(I32) << 8) + (part[2].astype(I32) << 16)
    for t in range(taylor):
        amps_ref[t * S:(t + 1) * S, :] = part[3 + 3 * t] + (part[4 + 3 * t] + part[5 + 3 * t])


def overlapping(lists, origin, *, patch, tile, taylor):
    S = lists.shape[0] // LIST
    return pl.pallas_call(
        functools.partial(list_kernel, patch=patch, tile=tile, taylor=taylor, origin=origin),
        out_shape=(jax.ShapeDtypeStruct((S + 8, LANES), I32), jax.ShapeDtypeStruct((taylor * S, LANES), F32)),
        in_specs=[vmem()], out_specs=(vmem(),) * 2,
        scratch_shapes=[pltpu.VMEM(((3 + 3 * taylor) * S, LANES), F32), pltpu.VMEM((S, LANES), I32)],
        compiler_params=pltpu.CompilerParams(vmem_limit_bytes=8 * 1024 * 1024),
    )(lists)


def render_kernel(words_ref, amps_ref, g_ref, gt_ref, dirty_hbm, res_ref, tay_ref,
                  words_s, amps_s, dirty_ref, acc, acct, sems, *, patch, tile, taylor, scales):
    rows = tile + 2 * patch
    S = words_ref.shape[0] - 8
    h = patch // 2
    copies = (pltpu.make_async_copy(words_ref, words_s, sems.at[0]),
              pltpu.make_async_copy(amps_ref, amps_s, sems.at[1]),
              pltpu.make_async_copy(dirty_hbm, dirty_ref, sems.at[2]))
    for copy in copies:
        copy.start()
    for j in range(1, acc.shape[0] // rows - 1):
        acc[pl.ds(j * rows + patch, tile), :] = jnp.zeros((tile, LANES), F32)
        acct[pl.ds(j * rows + patch - h, tile + h), :] = jnp.zeros((tile + h, LANES), F32)
    for copy in copies[:2]:
        copy.wait()
    n = words_s[S, 0]
    lane_half = lax.broadcasted_iota(I32, (1, LANES), 1) & (HALF - 1)

    def gen(it, k):
        row, col = it // (LANES // U), (it % (LANES // U)) * U + k
        word = words_s[row, col]
        base, turn, width = word & 16383, (word >> 14) & (LANES - 1), word >> 21
        gb, hb = pl.multiple_of(width * patch, 8), pl.multiple_of(width * h, 8)
        p = q = None
        for t in range(taylor):
            a = amps_s[row + t * S, col]
            x = a * g_ref[pl.ds(gb + t * scales * patch, patch), :]
            y = a * gt_ref[pl.ds(hb + t * scales * h, h), :]
            p, q = (x, y) if p is None else (p + x, q + y)
        p = p.astype(BF16).astype(F32)
        return pltpu.roll(p, turn, 1), pltpu.roll(q, turn, 1), base, turn & (HALF - 1)

    def put(p, q, base, turn):
        first = lane_half >= turn
        for ref, val, high in ((acc, p, patch), (acct, q, h)):
            here, right = pl.ds(base, high), pl.ds(base + rows, high)
            ref[here, :] = ref[here, :] + jnp.where(first, val, 0.0)
            ref[right, :] = ref[right, :] + jnp.where(first, 0.0, val)

    def step(i, carry):
        for item in [gen(i, k) for k in range(U)]:
            put(*item)
        return carry

    lax.fori_loop(0, (n + U - 1) // U, step, 0)

    copies[2].wait()
    left = lax.broadcasted_iota(I32, (tile, LANES), 1) < HALF
    for c in range(tile // LANES):
        j, cols = 2 * c + 1, slice(c * LANES, (c + 1) * LANES)

        def get(ref, jj, top):
            return ref[pl.ds(jj * rows + top, tile), :]

        x, y = get(acc, j, patch), get(acc, j + 1, patch)
        res_ref[0, :, cols] = dirty_ref[0, :, cols] - jnp.where(left, x, y)
        res_ref[1, :, cols] = dirty_ref[1, :, cols] - pltpu.roll(jnp.where(left, y, x), HALF, 1)
        up = jnp.where(left, get(acct, j, patch), get(acct, j + 1, patch))
        low = pltpu.roll(jnp.where(left, get(acct, j + 1, patch - h), get(acct, j, patch - h)), HALF, 1)
        tay_ref[0, :, cols] = up + low


def render(words, amps, g, gt, dirty, *, patch, taylor, scales):
    tile = dirty.shape[1]
    rows, tiles = tile + 2 * patch, tile // HALF + 2
    return pl.pallas_call(
        functools.partial(render_kernel, patch=patch, tile=tile, taylor=taylor, scales=scales),
        out_shape=(jax.ShapeDtypeStruct(dirty.shape, F32), jax.ShapeDtypeStruct((1,) + dirty.shape[1:], F32)),
        in_specs=[vmem()] * 4 + [pl.BlockSpec(memory_space=pltpu.HBM)], out_specs=(vmem(),) * 2,
        scratch_shapes=[
            pltpu.SMEM(words.shape, I32), pltpu.SMEM(amps.shape, F32), pltpu.VMEM(dirty.shape, F32),
            pltpu.VMEM((tiles * rows, LANES), F32), pltpu.VMEM((tiles * rows, LANES), F32),
            pltpu.SemaphoreType.DMA((3,))],
        compiler_params=pltpu.CompilerParams(vmem_limit_bytes=8 * 1024 * 1024),
    )(words, amps, g, gt, pltpu.with_memory_space_constraint(dirty, pltpu.HBM))


def finish_kernel(res_ref, total_ref, fit_ref, res_hbm, tay_hbm, tay_ref, sems):
    res = pltpu.make_async_copy(res_ref, res_hbm, sems.at[0])
    res.start()
    tay_ref[...] = total_ref[...] - fit_ref[...]
    tay = pltpu.make_async_copy(tay_ref, tay_hbm, sems.at[1])
    tay.start()
    res.wait()
    tay.wait()


def finish(residual, total, model_fit):
    return pl.pallas_call(
        finish_kernel,
        out_shape=(jax.ShapeDtypeStruct(residual.shape, F32), jax.ShapeDtypeStruct(total.shape, F32)),
        in_specs=[vmem()] * 3, out_specs=(pl.BlockSpec(memory_space=pltpu.HBM),) * 2,
        scratch_shapes=[pltpu.VMEM(total.shape, F32), pltpu.SemaphoreType.DMA((2,))],
        compiler_params=pltpu.CompilerParams(vmem_limit_bytes=4 * 1024 * 1024),
    )(residual, total, model_fit)


def per_device(dirty, psf, comp_tile, comp_offset, comp_scale, comp_amp, fit_weight):
    bands, tile = dirty.shape[0], dirty.shape[1]
    patch = math.isqrt(psf.shape[2])
    taylor = comp_amp.shape[1]
    scales = psf.shape[1] // taylor
    n_ty, n_tx, n_band = lax.axis_size("ty"), lax.axis_size("tx"), lax.axis_size("band")
    lift = 2.0 ** math.floor(math.log2(65504.0 / (bands * 30.0)))
    bits = [1 << n for n in range((n_tx - 1).bit_length())]
    bits += [n_tx << n for n in range(1, (n_ty - 1).bit_length())] + [n_tx]
    shares = 2

    def share():
        return lax.axis_index("ty") % 2

    lists, psi_send, psi_keep, dirty_send, dirty_keep, pairs = prep(
        dirty, psf, comp_tile, comp_offset, comp_scale, comp_amp, fit_weight,
        lambda: lax.axis_index("band"), share, shares, n_tx, n_band, lift)

    def across(value, bit):
        got = lax.ppermute(value.astype(jnp.float16), "band", [(i, i ^ bit) for i in range(n_band)])
        return got.astype(F32) * (1.0 / lift)

    def hop(value, bit):
        return lax.ppermute(value, ("ty", "tx"), [(i, i ^ bit) for i in range(n_ty * n_tx)])

    psi = psi_keep + across(psi_send, 1)
    total = dirty_keep + across(dirty_send, 1)
    band_bits = [1 << n for n in range(1, (n_band - 1).bit_length())]
    for n, bit in enumerate(band_bits):
        cut = psi.shape[0] // 2
        got = across(psi[cut:] * lift, bit)
        psi = psi[:cut] + got
    g = pack(pairs, patch)
    for bit in bits[:-1]:
        lists = jnp.concatenate([lists, hop(lists, bit)], 0)
    cut = lists.shape[0]
    got = hop(jnp.concatenate([lists, psi[0]], 0), bits[-1])
    lists = jnp.concatenate([lists, got[:cut]], 0)
    psi = jnp.concatenate([psi[0], got[cut:]], 0)
    words, amps = overlapping(
        lists, lambda: (lax.axis_index("ty") * tile, lax.axis_index("tx") * tile),
        patch=patch, tile=tile, taylor=taylor)
    for bit in band_bits:
        cut = total.shape[0] // 2
        total = total[:cut] + across(total[cut:] * lift, bit)
    residual, model_fit = render(
        words, amps, g, pack_fit(psi, psf.shape[1], patch, shares, lambda s: share() ^ s), dirty,
        patch=patch, taylor=taylor, scales=scales)
    return finish(residual, total, model_fit)


def solution(mesh):
    return jax.shard_map(
        per_device,
        mesh=mesh,
        in_specs=(
            P("band", "ty", "tx"),
            P("band", None, None),
            P(("ty", "tx"), None),
            P(("ty", "tx"), None),
            P(("ty", "tx")),
            P(("ty", "tx"), None),
            P("band", None),
        ),
        out_specs=(P("band", "ty", "tx"), P("band", "ty", "tx")),
        check_vma=False,
    )
```

```python
import functools
import math
import jax
import jax.numpy as jnp
from jax import lax
from jax.experimental import pallas as pl
from jax.experimental.pallas import tpu as pltpu
from jax.sharding import PartitionSpec as P

LANES = 128
HALF = 64
U = 16
LIST = 8
F32, BF16, I32 = jnp.float32, jnp.bfloat16, jnp.int32


def vmem():
    return pl.BlockSpec(memory_space=pltpu.VMEM)


def prep_kernel(w_hbm, tile_hbm, offset_hbm, scale_hbm, amp_hbm, dirty_hbm, psf_hbm,
                feat_ref, pay_ref, keep_ref, dsend_ref, dkeep_ref, pairs,
                w_ref, tile_ref, offset_ref, scale_ref, amp_ref, dirty_ref, psf_ref, sems, *,
                me, share, shares, n_tx, n_band, lift):
    copies = [pltpu.make_async_copy(src, dst, sems.at[i]) for i, (src, dst) in enumerate((
        (psf_hbm, psf_ref), (w_hbm, w_ref), (tile_hbm, tile_ref), (offset_hbm, offset_ref),
        (scale_hbm, scale_ref), (amp_hbm, amp_ref), (dirty_hbm, dirty_ref)))]
    for copy in copies:
        copy.start()
    bands, side = dirty_ref.shape[0], dirty_ref.shape[1]
    kk, flat = psf_ref.shape[0], psf_ref.shape[2]
    chunks = flat // LANES
    taylor = amp_ref.shape[0]
    me, share = me(), share()
    part, block = kk // shares, keep_ref.shape[1]
    copies[0].wait()
    copies[1].wait()
    for c in range(chunks):
        for k in range(kk):
            top = (c * kk + k) * bands
            pairs[top:top + bands, :] = psf_ref[k, :, c * LANES:(c + 1) * LANES].astype(F32)
    weights = [[w_ref[b, me ^ step] * (lift if step % 2 else 1.0) for b in range(bands)] for step in range(n_band)]
    for c in range(chunks):
        rows = [pairs[pl.ds((c * kk + share * part) * bands + b, part, stride=bands), :] for b in range(bands)]
        for step in range(n_band):
            total = weights[step][0] * rows[0]
            for b in range(1, bands):
                total = total + weights[step][b] * rows[b]
            (pay_ref if step % 2 else keep_ref)[step // 2, c * part:(c + 1) * part, :] = total
    spare = jnp.zeros((block - part * chunks, LANES), F32)
    for step in range(n_band):
        (pay_ref if step % 2 else keep_ref)[step // 2, part * chunks:, :] = spare
    for copy in copies[2:]:
        copy.wait()
    tile = tile_ref[0:1, :]
    feat_ref[0:1, :] = ((tile // n_tx) * side + offset_ref[0:1, :]).astype(F32)
    feat_ref[1:2, :] = ((tile % n_tx) * side + offset_ref[1:2, :]).astype(F32)
    feat_ref[2:3, :] = scale_ref[0:1, :].astype(F32)
    feat_ref[3:3 + taylor, :] = amp_ref[...]
    feat_ref[3 + taylor:, :] = jnp.zeros((LIST - 3 - taylor, LANES), F32)
    for step in range(n_band):
        total = weights[step][0] * dirty_ref[0]
        for b in range(1, bands):
            total = total + weights[step][b] * dirty_ref[b]
        (dsend_ref if step % 2 else dkeep_ref)[step // 2] = total


def prep(dirty, psf, comp_tile, comp_offset, comp_scale, comp_amp, fit_weight, me, share, shares, n_tx, n_band, lift):
    bands, kk, flat = psf.shape
    side = dirty.shape[1]
    chunks = flat // LANES
    block = -(-(kk // shares) * chunks // 16) * 16
    args = (fit_weight, comp_tile.T, comp_offset.T, comp_scale[None], comp_amp.T, dirty, psf.transpose(1, 0, 2))
    return pl.pallas_call(
        functools.partial(prep_kernel, me=me, share=share, shares=shares, n_tx=n_tx, n_band=n_band, lift=lift),
        out_shape=(
            jax.ShapeDtypeStruct((LIST, LANES), F32),
            jax.ShapeDtypeStruct((n_band // 2, block, LANES), F32),
            jax.ShapeDtypeStruct((n_band // 2, block, LANES), F32),
            jax.ShapeDtypeStruct((n_band // 2, side, side), F32),
            jax.ShapeDtypeStruct((n_band // 2, side, side), F32),
            jax.ShapeDtypeStruct((bands * kk * chunks, LANES), F32),
        ),
        in_specs=[pl.BlockSpec(memory_space=pltpu.HBM)] * len(args),
        out_specs=(vmem(),) * 6,
        scratch_shapes=[pltpu.SMEM(args[0].shape, F32)] + [pltpu.VMEM(x.shape, x.dtype) for x in args[1:]] + [
            pltpu.SemaphoreType.DMA((len(args),))],
        compiler_params=pltpu.CompilerParams(vmem_limit_bytes=12 * 1024 * 1024),
    )(*[pltpu.with_memory_space_constraint(x, pltpu.HBM) for x in args])


def pick(chunk, first, dest, lane, patch):
    c, off = divmod(first, LANES)
    a = chunk(c)
    if off + patch > LANES:
        a = jnp.where(lane >= off, a, chunk(c + 1))
    turn = (dest - off) % LANES
    return pltpu.roll(a, turn, 1) if turn else a


def pack_kernel(pairs_ref, out_ref, *, patch):
    kk = out_ref.shape[0] // patch
    lane = lax.broadcasted_iota(I32, (kk, LANES), 1)

    def chunk(b, c):
        return pairs_ref[pl.ds(c * 2 * kk + b, kk, stride=2), :]

    for u in range(patch):
        two = [pick(functools.partial(chunk, b), u * patch, b * HALF, lane, patch) for b in range(2)]
        v = jnp.where(lane < HALF, two[0], two[1])
        out_ref[pl.ds(u, kk, stride=patch), :] = jnp.where(lane % HALF < patch, v, 0.0)


def pack(pairs, patch):
    return pl.pallas_call(
        functools.partial(pack_kernel, patch=patch),
        out_shape=jax.ShapeDtypeStruct((pairs.shape[0] // 2 // (patch * patch // LANES) * patch, LANES), F32),
        in_specs=[vmem()], out_specs=vmem(),
        compiler_params=pltpu.CompilerParams(vmem_limit_bytes=4 * 1024 * 1024),
    )(pairs)


def pack_fit(psi_ref, out_ref, *, patch, shares, start):
    h = patch // 2
    n, block = out_ref.shape[0] // h // shares, psi_ref.shape[0] // shares
    lane = lax.broadcasted_iota(I32, (n, LANES), 1)
    for s in range(shares):
        top = start(s) * (n * h)

        def chunk(c):
            return psi_ref[s * block + c * n:s * block + (c + 1) * n, :]

        for u in range(h):
            v = jnp.where(lane < HALF, pick(chunk, u * patch, 0, lane, patch),
                          pick(chunk, (u + h) * patch, HALF, lane, patch))
            out_ref[pl.ds(top + u, n, stride=h), :] = jnp.where(lane % HALF < patch, v, 0.0)


def list_components(list_ref, words_ref, amps_ref, piece_v, rank_v, *, patch, tile, taylor, origin):
    rows = tile + 2 * patch
    S = list_ref.shape[0] // LIST

    def plane(n):
        return list_ref[pl.ds(n, S, stride=LIST), :]

    r0, c0 = origin()
    rr = plane(0).astype(I32) - r0
    cc = plane(1).astype(I32) - c0
    mask = (rr > -patch) & (rr < tile) & (cc > -patch) & (cc < tile)
    mb = jnp.where(mask, 1.0, 0.0).astype(BF16)
    i0 = lax.broadcasted_iota(I32, (LANES, LANES), 0)
    i1 = lax.broadcasted_iota(I32, (LANES, LANES), 1)
    upper = jnp.where(i0 < i1, 1.0, 0.0).astype(BF16)
    ones = jnp.ones((LANES, LANES), BF16)
    s0 = lax.broadcasted_iota(I32, (S, S), 0)
    s1 = lax.broadcasted_iota(I32, (S, S), 1)
    below = jnp.where(s1 < s0, 1.0, 0.0).astype(BF16)
    before = jnp.dot(below, mb, preferred_element_type=F32).astype(BF16)
    every = jnp.dot(jnp.ones((8, S), BF16), mb, preferred_element_type=F32).astype(BF16)
    rank = jnp.dot(mb, upper, preferred_element_type=F32) + jnp.dot(before, ones, preferred_element_type=F32)
    words_ref[S:S + 8, :] = jnp.dot(every, ones, preferred_element_type=F32).astype(I32)
    rank_v[...] = jnp.where(mask, rank, -1.0).astype(I32)
    base = jnp.where(mask, ((cc + HALF) >> 6) * rows + rr + patch, 0)
    word = base + ((cc & (LANES - 1)) << 14) + (plane(2).astype(I32) << 21)
    pieces = [(word & 255).astype(F32), ((word >> 8) & 255).astype(F32), ((word >> 16) & 255).astype(F32)]
    for t in range(taylor):
        rest = plane(3 + t)
        for _ in range(3):
            pieces.append(rest.astype(BF16).astype(F32))
            rest = rest - pieces[-1]
    for n, piece in enumerate(pieces):
        piece_v[n * S:(n + 1) * S, :] = piece
    srow = lax.broadcasted_iota(I32, (S, LANES), 0)

    def spread(d, got):
        rank = rank_v[pl.ds(d, 1), :]
        hit = (rank >> 7) == srow
        onehot = jnp.where((rank & (LANES - 1)) == i0, 1.0, 0.0).astype(BF16)
        lhs = jnp.concatenate([jnp.where(hit, piece_v[pl.ds(n * S + d, 1), :], 0.0) for n in range(len(pieces))], 0)
        return got + lax.dot_general(lhs.astype(BF16), onehot, (((1,), (1,)), ((), ())), preferred_element_type=F32)

    got = jnp.zeros((len(pieces) * S, LANES), F32)
    if S <= 16:
        for d in range(S):
            got = spread(d, got)
    else:
        got = lax.fori_loop(0, S, spread, got)
    part = [got[n * S:(n + 1) * S] for n in range(len(pieces))]
    words_ref[0:S, :] = part[0].astype(I32) + (part[1].astype(I32) << 8) + (part[2].astype(I32) << 16)
    for t in range(taylor):
        amps_ref[t * S:(t + 1) * S, :] = part[3 + 3 * t] + (part[4 + 3 * t] + part[5 + 3 * t])


def render_kernel(list_ref, psi_ref, g_ref, dirty_hbm, res_ref, tay_ref,
                  words_ref, amps_ref, piece_v, rank_v, gt_ref, words_s, amps_s, dirty_ref, acc, acct, sems, *,
                  patch, tile, taylor, scales, origin, shares, start):
    rows = tile + 2 * patch
    S = words_ref.shape[0] - 8
    h = patch // 2
    copies = (pltpu.make_async_copy(words_ref, words_s, sems.at[0]),
              pltpu.make_async_copy(amps_ref, amps_s, sems.at[1]),
              pltpu.make_async_copy(dirty_hbm, dirty_ref, sems.at[2]))
    copies[2].start()
    list_components(list_ref, words_ref, amps_ref, piece_v, rank_v,
                    patch=patch, tile=tile, taylor=taylor, origin=origin)
    copies[0].start()
    copies[1].start()
    pack_fit(psi_ref, gt_ref, patch=patch, shares=shares, start=start)
    for j in range(1, acc.shape[0] // rows - 1):
        acc[pl.ds(j * rows + patch, tile), :] = jnp.zeros((tile, LANES), F32)
        acct[pl.ds(j * rows + patch - h, tile + h), :] = jnp.zeros((tile + h, LANES), F32)
    for copy in copies[:2]:
        copy.wait()
    n = words_s[S, 0]
    lane_half = lax.broadcasted_iota(I32, (1, LANES), 1) & (HALF - 1)

    def gen(it, k):
        row, col = it // (LANES // U), (it % (LANES // U)) * U + k
        word = words_s[row, col]
        base, turn, width = word & 16383, (word >> 14) & (LANES - 1), word >> 21
        gb, hb = pl.multiple_of(width * patch, 8), pl.multiple_of(width * h, 8)
        p = q = None
        for t in range(taylor):
            a = amps_s[row + t * S, col]
            x = a * g_ref[pl.ds(gb + t * scales * patch, patch), :]
            y = a * gt_ref[pl.ds(hb + t * scales * h, h), :]
            p, q = (x, y) if p is None else (p + x, q + y)
        p = p.astype(BF16).astype(F32)
        return pltpu.roll(p, turn, 1), pltpu.roll(q, turn, 1), base, turn & (HALF - 1)

    def put(p, q, base, turn):
        first = lane_half >= turn
        for ref, val, high in ((acc, p, patch), (acct, q, h)):
            here, right = pl.ds(base, high), pl.ds(base + rows, high)
            ref[here, :] = ref[here, :] + jnp.where(first, val, 0.0)
            ref[right, :] = ref[right, :] + jnp.where(first, 0.0, val)

    def step(i, carry):
        for item in [gen(i, k) for k in range(U)]:
            put(*item)
        return carry

    lax.fori_loop(0, (n + U - 1) // U, step, 0)

    copies[2].wait()
    left = lax.broadcasted_iota(I32, (tile, LANES), 1) < HALF
    for c in range(tile // LANES):
        j, cols = 2 * c + 1, slice(c * LANES, (c + 1) * LANES)

        def get(ref, jj, top):
            return ref[pl.ds(jj * rows + top, tile), :]

        x, y = get(acc, j, patch), get(acc, j + 1, patch)
        res_ref[0, :, cols] = dirty_ref[0, :, cols] - jnp.where(left, x, y)
        res_ref[1, :, cols] = dirty_ref[1, :, cols] - pltpu.roll(jnp.where(left, y, x), HALF, 1)
        up = jnp.where(left, get(acct, j, patch), get(acct, j + 1, patch))
        low = pltpu.roll(jnp.where(left, get(acct, j + 1, patch - h), get(acct, j, patch - h)), HALF, 1)
        tay_ref[0, :, cols] = up + low


def render(lists, psi, g, dirty, origin, start, *, patch, taylor, scales, shares):
    tile, S = dirty.shape[1], lists.shape[0] // LIST
    rows, tiles = tile + 2 * patch, tile // HALF + 2
    return pl.pallas_call(
        functools.partial(render_kernel, patch=patch, tile=tile, taylor=taylor, scales=scales,
                          origin=origin, shares=shares, start=start),
        out_shape=(jax.ShapeDtypeStruct(dirty.shape, F32), jax.ShapeDtypeStruct((1,) + dirty.shape[1:], F32)),
        in_specs=[vmem()] * 3 + [pl.BlockSpec(memory_space=pltpu.HBM)], out_specs=(vmem(),) * 2,
        scratch_shapes=[
            pltpu.VMEM((S + 8, LANES), I32), pltpu.VMEM((taylor * S, LANES), F32),
            pltpu.VMEM(((3 + 3 * taylor) * S, LANES), F32), pltpu.VMEM((S, LANES), I32),
            pltpu.VMEM((g.shape[0] // 2, LANES), F32),
            pltpu.SMEM((S + 8, LANES), I32), pltpu.SMEM((taylor * S, LANES), F32), pltpu.VMEM(dirty.shape, F32),
            pltpu.VMEM((tiles * rows, LANES), F32), pltpu.VMEM((tiles * rows, LANES), F32),
            pltpu.SemaphoreType.DMA((3,))],
        compiler_params=pltpu.CompilerParams(vmem_limit_bytes=12 * 1024 * 1024),
    )(lists, psi, g, pltpu.with_memory_space_constraint(dirty, pltpu.HBM))


def finish_kernel(res_ref, total_ref, fit_ref, res_hbm, tay_hbm, tay_ref, sems):
    res = pltpu.make_async_copy(res_ref, res_hbm, sems.at[0])
    res.start()
    tay_ref[...] = total_ref[...] - fit_ref[...]
    tay = pltpu.make_async_copy(tay_ref, tay_hbm, sems.at[1])
    tay.start()
    res.wait()
    tay.wait()


def finish(residual, total, model_fit):
    return pl.pallas_call(
        finish_kernel,
        out_shape=(jax.ShapeDtypeStruct(residual.shape, F32), jax.ShapeDtypeStruct(total.shape, F32)),
        in_specs=[vmem()] * 3, out_specs=(pl.BlockSpec(memory_space=pltpu.HBM),) * 2,
        scratch_shapes=[pltpu.VMEM(total.shape, F32), pltpu.SemaphoreType.DMA((2,))],
        compiler_params=pltpu.CompilerParams(vmem_limit_bytes=4 * 1024 * 1024),
    )(residual, total, model_fit)


def per_device(dirty, psf, comp_tile, comp_offset, comp_scale, comp_amp, fit_weight):
    bands, tile = dirty.shape[0], dirty.shape[1]
    patch = math.isqrt(psf.shape[2])
    taylor = comp_amp.shape[1]
    scales = psf.shape[1] // taylor
    n_ty, n_tx, n_band = lax.axis_size("ty"), lax.axis_size("tx"), lax.axis_size("band")
    lift = 2.0 ** math.floor(math.log2(65504.0 / (bands * 30.0)))
    bits = [1 << n for n in range((n_tx - 1).bit_length())]
    bits += [n_tx << n for n in range(1, (n_ty - 1).bit_length())] + [n_tx]
    shares = 2

    def share():
        return lax.axis_index("ty") % 2

    lists, psi_send, psi_keep, dirty_send, dirty_keep, pairs = prep(
        dirty, psf, comp_tile, comp_offset, comp_scale, comp_amp, fit_weight,
        lambda: lax.axis_index("band"), share, shares, n_tx, n_band, lift)

    def across(value, bit):
        got = lax.ppermute(value.astype(jnp.float16), "band", [(i, i ^ bit) for i in range(n_band)])
        return got.astype(F32) * (1.0 / lift)

    def hop(value, bit):
        return lax.ppermute(value, ("ty", "tx"), [(i, i ^ bit) for i in range(n_ty * n_tx)])

    psi = psi_keep + across(psi_send, 1)
    total = dirty_keep + across(dirty_send, 1)
    band_bits = [1 << n for n in range(1, (n_band - 1).bit_length())]
    for n, bit in enumerate(band_bits):
        cut = psi.shape[0] // 2
        got = across(psi[cut:] * lift, bit)
        psi = psi[:cut] + got
    g = pack(pairs, patch)
    for bit in bits[:-1]:
        lists = jnp.concatenate([lists, hop(lists, bit)], 0)
    cut = lists.shape[0]
    got = hop(jnp.concatenate([lists, psi[0]], 0), bits[-1])
    lists = jnp.concatenate([lists, got[:cut]], 0)
    psi = jnp.concatenate([psi[0], got[cut:]], 0)
    for bit in band_bits:
        cut = total.shape[0] // 2
        total = total[:cut] + across(total[cut:] * lift, bit)
    residual, model_fit = render(
        lists, psi, g, dirty, lambda: (lax.axis_index("ty") * tile, lax.axis_index("tx") * tile),
        lambda s: share() ^ s, patch=patch, taylor=taylor, scales=scales, shares=shares)
    return finish(residual, total, model_fit)


def solution(mesh):
    return jax.shard_map(
        per_device,
        mesh=mesh,
        in_specs=(
            P("band", "ty", "tx"),
            P("band", None, None),
            P(("ty", "tx"), None),
            P(("ty", "tx"), None),
            P(("ty", "tx")),
            P(("ty", "tx"), None),
            P("band", None),
        ),
        out_specs=(P("band", "ty", "tx"), P("band", "ty", "tx")),
        check_vma=False,
    )
```

```python
import functools
import math
import jax
import jax.numpy as jnp
from jax import lax
from jax.experimental import pallas as pl
from jax.experimental.pallas import tpu as pltpu
from jax.sharding import PartitionSpec as P

LANES = 128
HALF = 64
U = 16
LIST = 8
F32, BF16, I32 = jnp.float32, jnp.bfloat16, jnp.int32


def vmem():
    return pl.BlockSpec(memory_space=pltpu.VMEM)


def prep_kernel(w_hbm, tile_hbm, offset_hbm, scale_hbm, amp_hbm, dirty_hbm, psf_hbm,
                feat_ref, pay_ref, keep_ref, dsend_ref, dkeep_ref, pairs,
                w_ref, tile_ref, offset_ref, scale_ref, amp_ref, dirty_ref, psf_ref, sems, *,
                me, share, shares, n_tx, n_band, lift):
    copies = [pltpu.make_async_copy(src, dst, sems.at[i]) for i, (src, dst) in enumerate((
        (psf_hbm, psf_ref), (w_hbm, w_ref), (tile_hbm, tile_ref), (offset_hbm, offset_ref),
        (scale_hbm, scale_ref), (amp_hbm, amp_ref), (dirty_hbm, dirty_ref)))]
    for copy in copies:
        copy.start()
    bands, side = dirty_ref.shape[0], dirty_ref.shape[1]
    kk, flat = psf_ref.shape[0], psf_ref.shape[2]
    chunks = flat // LANES
    taylor = amp_ref.shape[0]
    me, share = me(), share()
    part, block = kk // shares, keep_ref.shape[1]
    copies[0].wait()
    copies[1].wait()
    for c in range(chunks):
        for k in range(kk):
            top = (c * kk + k) * bands
            pairs[top:top + bands, :] = psf_ref[k, :, c * LANES:(c + 1) * LANES].astype(F32)
    weights = [[w_ref[b, me ^ step] * (lift if step % 2 else 1.0) for b in range(bands)] for step in range(n_band)]
    for c in range(chunks):
        rows = [pairs[pl.ds((c * kk + share * part) * bands + b, part, stride=bands), :] for b in range(bands)]
        for step in range(n_band):
            total = weights[step][0] * rows[0]
            for b in range(1, bands):
                total = total + weights[step][b] * rows[b]
            (pay_ref if step % 2 else keep_ref)[step // 2, c * part:(c + 1) * part, :] = total
    spare = jnp.zeros((block - part * chunks, LANES), F32)
    for step in range(n_band):
        (pay_ref if step % 2 else keep_ref)[step // 2, part * chunks:, :] = spare
    for copy in copies[2:]:
        copy.wait()
    tile = tile_ref[0:1, :]
    feat_ref[0:1, :] = ((tile // n_tx) * side + offset_ref[0:1, :]).astype(F32)
    feat_ref[1:2, :] = ((tile % n_tx) * side + offset_ref[1:2, :]).astype(F32)
    feat_ref[2:3, :] = scale_ref[0:1, :].astype(F32)
    feat_ref[3:3 + taylor, :] = amp_ref[...]
    feat_ref[3 + taylor:, :] = jnp.zeros((LIST - 3 - taylor, LANES), F32)
    for step in range(n_band):
        total = weights[step][0] * dirty_ref[0]
        for b in range(1, bands):
            total = total + weights[step][b] * dirty_ref[b]
        (dsend_ref if step % 2 else dkeep_ref)[step // 2] = total


def prep(dirty, psf, comp_tile, comp_offset, comp_scale, comp_amp, fit_weight, me, share, shares, n_tx, n_band, lift):
    bands, kk, flat = psf.shape
    side = dirty.shape[1]
    chunks = flat // LANES
    block = -(-(kk // shares) * chunks // 16) * 16
    args = (fit_weight, comp_tile.T, comp_offset.T, comp_scale[None], comp_amp.T, dirty, psf.transpose(1, 0, 2))
    return pl.pallas_call(
        functools.partial(prep_kernel, me=me, share=share, shares=shares, n_tx=n_tx, n_band=n_band, lift=lift),
        out_shape=(
            jax.ShapeDtypeStruct((LIST, LANES), F32),
            jax.ShapeDtypeStruct((n_band // 2, block, LANES), F32),
            jax.ShapeDtypeStruct((n_band // 2, block, LANES), F32),
            jax.ShapeDtypeStruct((n_band // 2, side, side), F32),
            jax.ShapeDtypeStruct((n_band // 2, side, side), F32),
            jax.ShapeDtypeStruct((bands * kk * chunks, LANES), F32),
        ),
        in_specs=[pl.BlockSpec(memory_space=pltpu.HBM)] * len(args),
        out_specs=(vmem(),) * 6,
        scratch_shapes=[pltpu.SMEM(args[0].shape, F32)] + [pltpu.VMEM(x.shape, x.dtype) for x in args[1:]] + [
            pltpu.SemaphoreType.DMA((len(args),))],
        compiler_params=pltpu.CompilerParams(vmem_limit_bytes=12 * 1024 * 1024),
    )(*[pltpu.with_memory_space_constraint(x, pltpu.HBM) for x in args])


def pick(chunk, first, dest, lane, patch):
    c, off = divmod(first, LANES)
    a = chunk(c)
    if off + patch > LANES:
        a = jnp.where(lane >= off, a, chunk(c + 1))
    turn = (dest - off) % LANES
    return pltpu.roll(a, turn, 1) if turn else a


def pack_kernel(pairs_ref, out_ref, *, patch):
    kk = out_ref.shape[0] // patch
    lane = lax.broadcasted_iota(I32, (kk, LANES), 1)

    def chunk(b, c):
        return pairs_ref[pl.ds(c * 2 * kk + b, kk, stride=2), :]

    for u in range(patch):
        two = [pick(functools.partial(chunk, b), u * patch, b * HALF, lane, patch) for b in range(2)]
        v = jnp.where(lane < HALF, two[0], two[1])
        out_ref[pl.ds(u, kk, stride=patch), :] = jnp.where(lane % HALF < patch, v, 0.0)


def pack(pairs, patch):
    return pl.pallas_call(
        functools.partial(pack_kernel, patch=patch),
        out_shape=jax.ShapeDtypeStruct((pairs.shape[0] // 2 // (patch * patch // LANES) * patch, LANES), F32),
        in_specs=[vmem()], out_specs=vmem(),
        compiler_params=pltpu.CompilerParams(vmem_limit_bytes=4 * 1024 * 1024),
    )(pairs)


def pack_fit(psi_ref, out_ref, *, patch, shares, start):
    h = patch // 2
    n, block = out_ref.shape[0] // h // shares, psi_ref.shape[0] // shares
    lane = lax.broadcasted_iota(I32, (n, LANES), 1)
    for s in range(shares):
        top = start(s) * (n * h)

        def chunk(c):
            return psi_ref[s * block + c * n:s * block + (c + 1) * n, :]

        for u in range(h):
            v = jnp.where(lane < HALF, pick(chunk, u * patch, 0, lane, patch),
                          pick(chunk, (u + h) * patch, HALF, lane, patch))
            out_ref[pl.ds(top + u, n, stride=h), :] = jnp.where(lane % HALF < patch, v, 0.0)


def list_components(list_ref, words_ref, amps_ref, piece_v, rank_v, *, patch, tile, taylor, origin):
    rows = tile + 2 * patch
    S = list_ref.shape[0] // LIST

    def plane(n):
        return list_ref[pl.ds(n, S, stride=LIST), :]

    r0, c0 = origin()
    rr = plane(0).astype(I32) - r0
    cc = plane(1).astype(I32) - c0
    mask = (rr > -patch) & (rr < tile) & (cc > -patch) & (cc < tile)
    mb = jnp.where(mask, 1.0, 0.0).astype(BF16)
    i0 = lax.broadcasted_iota(I32, (LANES, LANES), 0)
    i1 = lax.broadcasted_iota(I32, (LANES, LANES), 1)
    upper = jnp.where(i0 < i1, 1.0, 0.0).astype(BF16)
    ones = jnp.ones((LANES, LANES), BF16)
    s0 = lax.broadcasted_iota(I32, (S, S), 0)
    s1 = lax.broadcasted_iota(I32, (S, S), 1)
    below = jnp.where(s1 < s0, 1.0, 0.0).astype(BF16)
    before = jnp.dot(below, mb, preferred_element_type=F32).astype(BF16)
    every = jnp.dot(jnp.ones((8, S), BF16), mb, preferred_element_type=F32).astype(BF16)
    rank = jnp.dot(mb, upper, preferred_element_type=F32) + jnp.dot(before, ones, preferred_element_type=F32)
    words_ref[S:S + 8, :] = jnp.dot(every, ones, preferred_element_type=F32).astype(I32)
    rank_v[...] = jnp.where(mask, rank, -1.0).astype(I32)
    base = jnp.where(mask, ((cc + HALF) >> 6) * rows + rr + patch, 0)
    word = base + ((cc & (LANES - 1)) << 14) + (plane(2).astype(I32) << 21)
    pieces = [(word & 255).astype(F32), ((word >> 8) & 255).astype(F32), ((word >> 16) & 255).astype(F32)]
    for t in range(taylor):
        rest = plane(3 + t)
        for _ in range(3):
            pieces.append(rest.astype(BF16).astype(F32))
            rest = rest - pieces[-1]
    for n, piece in enumerate(pieces):
        piece_v[n * S:(n + 1) * S, :] = piece
    srow = lax.broadcasted_iota(I32, (S, LANES), 0)

    def spread(d, got):
        rank = rank_v[pl.ds(d, 1), :]
        hit = (rank >> 7) == srow
        onehot = jnp.where((rank & (LANES - 1)) == i0, 1.0, 0.0).astype(BF16)
        lhs = jnp.concatenate([jnp.where(hit, piece_v[pl.ds(n * S + d, 1), :], 0.0) for n in range(len(pieces))], 0)
        return got + lax.dot_general(lhs.astype(BF16), onehot, (((1,), (1,)), ((), ())), preferred_element_type=F32)

    got = jnp.zeros((len(pieces) * S, LANES), F32)
    if S <= 16:
        for d in range(S):
            got = spread(d, got)
    else:
        got = lax.fori_loop(0, S, spread, got)
    part = [got[n * S:(n + 1) * S] for n in range(len(pieces))]
    words_ref[0:S, :] = part[0].astype(I32) + (part[1].astype(I32) << 8) + (part[2].astype(I32) << 16)
    for t in range(taylor):
        amps_ref[t * S:(t + 1) * S, :] = part[3 + 3 * t] + (part[4 + 3 * t] + part[5 + 3 * t])


def render_kernel(list_ref, psi_ref, g_ref, dirty_hbm, res_ref, tay_ref,
                  words_ref, amps_ref, piece_v, rank_v, gt_ref, words_s, amps_s, dirty_ref, acc, acct, sems, *,
                  patch, tile, taylor, scales, origin, shares, start):
    rows = tile + 2 * patch
    S = words_ref.shape[0] - 8
    h = patch // 2
    copies = (pltpu.make_async_copy(words_ref, words_s, sems.at[0]),
              pltpu.make_async_copy(amps_ref, amps_s, sems.at[1]),
              pltpu.make_async_copy(dirty_hbm, dirty_ref, sems.at[2]))
    copies[2].start()
    list_components(list_ref, words_ref, amps_ref, piece_v, rank_v,
                    patch=patch, tile=tile, taylor=taylor, origin=origin)
    copies[0].start()
    copies[1].start()
    pack_fit(psi_ref, gt_ref, patch=patch, shares=shares, start=start)
    for j in range(1, acc.shape[0] // rows - 1):
        acc[pl.ds(j * rows + patch, tile), :] = jnp.zeros((tile, LANES), F32)
        acct[pl.ds(j * rows + patch - h, tile + h), :] = jnp.zeros((tile + h, LANES), F32)
    for copy in copies[:2]:
        copy.wait()
    n = words_s[S, 0]
    lane_half = lax.broadcasted_iota(I32, (1, LANES), 1) & (HALF - 1)

    def gen(it, k):
        row, col = it // (LANES // U), (it % (LANES // U)) * U + k
        word = words_s[row, col]
        base, turn, width = word & 16383, (word >> 14) & (LANES - 1), word >> 21
        gb, hb = pl.multiple_of(width * patch, 8), pl.multiple_of(width * h, 8)
        p = q = None
        for t in range(taylor):
            a = amps_s[row + t * S, col]
            x = a * g_ref[pl.ds(gb + t * scales * patch, patch), :]
            y = a * gt_ref[pl.ds(hb + t * scales * h, h), :]
            p, q = (x, y) if p is None else (p + x, q + y)
        p = p.astype(BF16).astype(F32)
        return pltpu.roll(p, turn, 1), pltpu.roll(q, turn, 1), base, turn & (HALF - 1)

    def put(p, q, base, turn):
        first = lane_half >= turn
        for ref, val, high in ((acc, p, patch), (acct, q, h)):
            here, right = pl.ds(base, high), pl.ds(base + rows, high)
            ref[here, :] = ref[here, :] + jnp.where(first, val, 0.0)
            ref[right, :] = ref[right, :] + jnp.where(first, 0.0, val)

    def step(i, carry):
        for item in [gen(i, k) for k in range(U)]:
            put(*item)
        return carry

    lax.fori_loop(0, (n + U - 1) // U, step, 0)

    copies[2].wait()
    left = lax.broadcasted_iota(I32, (tile, LANES), 1) < HALF
    for c in range(tile // LANES):
        j, cols = 2 * c + 1, slice(c * LANES, (c + 1) * LANES)

        def get(ref, jj, top):
            return ref[pl.ds(jj * rows + top, tile), :]

        x, y = get(acc, j, patch), get(acc, j + 1, patch)
        res_ref[0, :, cols] = dirty_ref[0, :, cols] - jnp.where(left, x, y)
        res_ref[1, :, cols] = dirty_ref[1, :, cols] - pltpu.roll(jnp.where(left, y, x), HALF, 1)
        up = jnp.where(left, get(acct, j, patch), get(acct, j + 1, patch))
        low = pltpu.roll(jnp.where(left, get(acct, j + 1, patch - h), get(acct, j, patch - h)), HALF, 1)
        tay_ref[0, :, cols] = up + low


def render(lists, psi, g, dirty, origin, start, *, patch, taylor, scales, shares):
    tile, S = dirty.shape[1], lists.shape[0] // LIST
    rows, tiles = tile + 2 * patch, tile // HALF + 2
    return pl.pallas_call(
        functools.partial(render_kernel, patch=patch, tile=tile, taylor=taylor, scales=scales,
                          origin=origin, shares=shares, start=start),
        out_shape=(jax.ShapeDtypeStruct(dirty.shape, F32), jax.ShapeDtypeStruct((1,) + dirty.shape[1:], F32)),
        in_specs=[vmem()] * 3 + [pl.BlockSpec(memory_space=pltpu.HBM)], out_specs=(vmem(),) * 2,
        scratch_shapes=[
            pltpu.VMEM((S + 8, LANES), I32), pltpu.VMEM((taylor * S, LANES), F32),
            pltpu.VMEM(((3 + 3 * taylor) * S, LANES), F32), pltpu.VMEM((S, LANES), I32),
            pltpu.VMEM((g.shape[0] // 2, LANES), F32),
            pltpu.SMEM((S + 8, LANES), I32), pltpu.SMEM((taylor * S, LANES), F32), pltpu.VMEM(dirty.shape, F32),
            pltpu.VMEM((tiles * rows, LANES), F32), pltpu.VMEM((tiles * rows, LANES), F32),
            pltpu.SemaphoreType.DMA((3,))],
        compiler_params=pltpu.CompilerParams(vmem_limit_bytes=12 * 1024 * 1024),
    )(lists, psi, g, pltpu.with_memory_space_constraint(dirty, pltpu.HBM))


def write_kernel(value_ref, out_hbm, sem):
    copy = pltpu.make_async_copy(value_ref, out_hbm, sem)
    copy.start()
    copy.wait()


def written(value):
    return pl.pallas_call(
        write_kernel,
        out_shape=jax.ShapeDtypeStruct(value.shape, F32),
        in_specs=[vmem()], out_specs=pl.BlockSpec(memory_space=pltpu.HBM),
        scratch_shapes=[pltpu.SemaphoreType.DMA],
        compiler_params=pltpu.CompilerParams(vmem_limit_bytes=4 * 1024 * 1024),
    )(value)


def per_device(dirty, psf, comp_tile, comp_offset, comp_scale, comp_amp, fit_weight):
    bands, tile = dirty.shape[0], dirty.shape[1]
    patch = math.isqrt(psf.shape[2])
    taylor = comp_amp.shape[1]
    scales = psf.shape[1] // taylor
    n_ty, n_tx, n_band = lax.axis_size("ty"), lax.axis_size("tx"), lax.axis_size("band")
    lift = 2.0 ** math.floor(math.log2(65504.0 / (bands * 30.0)))
    bits = [1 << n for n in range((n_tx - 1).bit_length())]
    bits += [n_tx << n for n in range(1, (n_ty - 1).bit_length())] + [n_tx]
    shares = 2

    def share():
        return lax.axis_index("ty") % 2

    lists, psi_send, psi_keep, dirty_send, dirty_keep, pairs = prep(
        dirty, psf, comp_tile, comp_offset, comp_scale, comp_amp, fit_weight,
        lambda: lax.axis_index("band"), share, shares, n_tx, n_band, lift)

    def across(value, bit):
        got = lax.ppermute(value.astype(jnp.float16), "band", [(i, i ^ bit) for i in range(n_band)])
        return got.astype(F32) * (1.0 / lift)

    def hop(value, bit):
        return lax.ppermute(value, ("ty", "tx"), [(i, i ^ bit) for i in range(n_ty * n_tx)])

    psi = psi_keep + across(psi_send, 1)
    total = dirty_keep + across(dirty_send, 1)
    band_bits = [1 << n for n in range(1, (n_band - 1).bit_length())]
    for n, bit in enumerate(band_bits):
        cut = psi.shape[0] // 2
        got = across(psi[cut:] * lift, bit)
        psi = psi[:cut] + got
    g = pack(pairs, patch)
    for bit in bits[:-1]:
        lists = jnp.concatenate([lists, hop(lists, bit)], 0)
    cut = lists.shape[0]
    got = hop(jnp.concatenate([lists, psi[0]], 0), bits[-1])
    lists = jnp.concatenate([lists, got[:cut]], 0)
    psi = jnp.concatenate([psi[0], got[cut:]], 0)
    for bit in band_bits:
        cut = total.shape[0] // 2
        total = total[:cut] + across(total[cut:] * lift, bit)
    residual, model_fit = render(
        lists, psi, g, dirty, lambda: (lax.axis_index("ty") * tile, lax.axis_index("tx") * tile),
        lambda s: share() ^ s, patch=patch, taylor=taylor, scales=scales, shares=shares)
    return written(residual), total - model_fit


def solution(mesh):
    return jax.shard_map(
        per_device,
        mesh=mesh,
        in_specs=(
            P("band", "ty", "tx"),
            P("band", None, None),
            P(("ty", "tx"), None),
            P(("ty", "tx"), None),
            P(("ty", "tx")),
            P(("ty", "tx"), None),
            P("band", None),
        ),
        out_specs=(P("band", "ty", "tx"), P("band", "ty", "tx")),
        check_vma=False,
    )
```

```python
import functools
import math
import jax
import jax.numpy as jnp
from jax import lax
from jax.experimental import pallas as pl
from jax.experimental.pallas import tpu as pltpu
from jax.sharding import PartitionSpec as P

LANES = 128
HALF = 64
U = 16
LIST = 8
F32, BF16, I32 = jnp.float32, jnp.bfloat16, jnp.int32


def vmem():
    return pl.BlockSpec(memory_space=pltpu.VMEM)


def prep_kernel(w_hbm, tile_hbm, offset_hbm, scale_hbm, amp_hbm, dirty_hbm, psf_hbm,
                feat_ref, pay_ref, keep_ref, dsend_ref, dkeep_ref, pairs,
                w_ref, tile_ref, offset_ref, scale_ref, amp_ref, dirty_ref, psf_ref, sems, *,
                me, share, shares, n_tx, n_band, lift):
    copies = [pltpu.make_async_copy(src, dst, sems.at[i]) for i, (src, dst) in enumerate((
        (psf_hbm, psf_ref), (w_hbm, w_ref), (tile_hbm, tile_ref), (offset_hbm, offset_ref),
        (scale_hbm, scale_ref), (amp_hbm, amp_ref), (dirty_hbm, dirty_ref)))]
    for copy in copies:
        copy.start()
    bands, side = dirty_ref.shape[0], dirty_ref.shape[1]
    kk, flat = psf_ref.shape[0], psf_ref.shape[2]
    chunks = flat // LANES
    taylor = amp_ref.shape[0]
    me, share = me(), share()
    part, block = kk // shares, keep_ref.shape[1]
    copies[0].wait()
    copies[1].wait()
    for c in range(chunks):
        for k in range(kk):
            top = (c * kk + k) * bands
            pairs[top:top + bands, :] = psf_ref[k, :, c * LANES:(c + 1) * LANES].astype(F32)
    weights = [[w_ref[b, me ^ step] * (lift if step % 2 else 1.0) for b in range(bands)] for step in range(n_band)]
    for c in range(chunks):
        rows = [pairs[pl.ds((c * kk + share * part) * bands + b, part, stride=bands), :] for b in range(bands)]
        for step in range(n_band):
            total = weights[step][0] * rows[0]
            for b in range(1, bands):
                total = total + weights[step][b] * rows[b]
            (pay_ref if step % 2 else keep_ref)[step // 2, c * part:(c + 1) * part, :] = total
    spare = jnp.zeros((block - part * chunks, LANES), F32)
    for step in range(n_band):
        (pay_ref if step % 2 else keep_ref)[step // 2, part * chunks:, :] = spare
    for copy in copies[2:]:
        copy.wait()
    tile = tile_ref[0:1, :]
    feat_ref[0:1, :] = ((tile // n_tx) * side + offset_ref[0:1, :]).astype(F32)
    feat_ref[1:2, :] = ((tile % n_tx) * side + offset_ref[1:2, :]).astype(F32)
    feat_ref[2:3, :] = scale_ref[0:1, :].astype(F32)
    feat_ref[3:3 + taylor, :] = amp_ref[...]
    feat_ref[3 + taylor:, :] = jnp.zeros((LIST - 3 - taylor, LANES), F32)
    for step in range(n_band):
        total = weights[step][0] * dirty_ref[0]
        for b in range(1, bands):
            total = total + weights[step][b] * dirty_ref[b]
        (dsend_ref if step % 2 else dkeep_ref)[step // 2] = total


def prep(dirty, psf, comp_tile, comp_offset, comp_scale, comp_amp, fit_weight, me, share, shares, n_tx, n_band, lift):
    bands, kk, flat = psf.shape
    side = dirty.shape[1]
    chunks = flat // LANES
    block = -(-(kk // shares) * chunks // 16) * 16
    args = (fit_weight, comp_tile.T, comp_offset.T, comp_scale[None], comp_amp.T, dirty, psf.transpose(1, 0, 2))
    return pl.pallas_call(
        functools.partial(prep_kernel, me=me, share=share, shares=shares, n_tx=n_tx, n_band=n_band, lift=lift),
        out_shape=(
            jax.ShapeDtypeStruct((LIST, LANES), F32),
            jax.ShapeDtypeStruct((n_band // 2, block, LANES), F32),
            jax.ShapeDtypeStruct((n_band // 2, block, LANES), F32),
            jax.ShapeDtypeStruct((n_band // 2, side, side), F32),
            jax.ShapeDtypeStruct((n_band // 2, side, side), F32),
            jax.ShapeDtypeStruct((bands * kk * chunks, LANES), F32),
        ),
        in_specs=[pl.BlockSpec(memory_space=pltpu.HBM)] * len(args),
        out_specs=(vmem(),) * 6,
        scratch_shapes=[pltpu.SMEM(args[0].shape, F32)] + [pltpu.VMEM(x.shape, x.dtype) for x in args[1:]] + [
            pltpu.SemaphoreType.DMA((len(args),))],
        compiler_params=pltpu.CompilerParams(vmem_limit_bytes=12 * 1024 * 1024),
    )(*[pltpu.with_memory_space_constraint(x, pltpu.HBM) for x in args])


def pick(chunk, first, dest, lane, patch):
    c, off = divmod(first, LANES)
    a = chunk(c)
    if off + patch > LANES:
        a = jnp.where(lane >= off, a, chunk(c + 1))
    turn = (dest - off) % LANES
    return pltpu.roll(a, turn, 1) if turn else a


def pack_kernel(pairs_ref, out_ref, *, patch):
    kk = out_ref.shape[0] // patch
    lane = lax.broadcasted_iota(I32, (kk, LANES), 1)

    def chunk(b, c):
        return pairs_ref[pl.ds(c * 2 * kk + b, kk, stride=2), :]

    for u in range(patch):
        two = [pick(functools.partial(chunk, b), u * patch, b * HALF, lane, patch) for b in range(2)]
        v = jnp.where(lane < HALF, two[0], two[1])
        out_ref[pl.ds(u, kk, stride=patch), :] = jnp.where(lane % HALF < patch, v, 0.0)


def pack(pairs, patch):
    return pl.pallas_call(
        functools.partial(pack_kernel, patch=patch),
        out_shape=jax.ShapeDtypeStruct((pairs.shape[0] // 2 // (patch * patch // LANES) * patch, LANES), F32),
        in_specs=[vmem()], out_specs=vmem(),
        compiler_params=pltpu.CompilerParams(vmem_limit_bytes=4 * 1024 * 1024),
    )(pairs)


def pack_fit(psi_ref, out_ref, *, patch, shares, start):
    h = patch // 2
    n, block = out_ref.shape[0] // h // shares, psi_ref.shape[0] // shares
    lane = lax.broadcasted_iota(I32, (n, LANES), 1)
    for s in range(shares):
        top = start(s) * (n * h)

        def chunk(c):
            return psi_ref[s * block + c * n:s * block + (c + 1) * n, :]

        for u in range(h):
            v = jnp.where(lane < HALF, pick(chunk, u * patch, 0, lane, patch),
                          pick(chunk, (u + h) * patch, HALF, lane, patch))
            out_ref[pl.ds(top + u, n, stride=h), :] = jnp.where(lane % HALF < patch, v, 0.0)


def list_components(list_ref, words_ref, amps_ref, piece_v, rank_v, *, patch, tile, taylor, origin):
    rows = tile + 2 * patch
    S = list_ref.shape[0] // LIST

    def plane(n):
        return list_ref[pl.ds(n, S, stride=LIST), :]

    r0, c0 = origin()
    rr = plane(0).astype(I32) - r0
    cc = plane(1).astype(I32) - c0
    mask = (rr > -patch) & (rr < tile) & (cc > -patch) & (cc < tile)
    mb = jnp.where(mask, 1.0, 0.0).astype(BF16)
    i0 = lax.broadcasted_iota(I32, (LANES, LANES), 0)
    i1 = lax.broadcasted_iota(I32, (LANES, LANES), 1)
    upper = jnp.where(i0 < i1, 1.0, 0.0).astype(BF16)
    ones = jnp.ones((LANES, LANES), BF16)
    s0 = lax.broadcasted_iota(I32, (S, S), 0)
    s1 = lax.broadcasted_iota(I32, (S, S), 1)
    below = jnp.where(s1 < s0, 1.0, 0.0).astype(BF16)
    before = jnp.dot(below, mb, preferred_element_type=F32).astype(BF16)
    every = jnp.dot(jnp.ones((8, S), BF16), mb, preferred_element_type=F32).astype(BF16)
    rank = jnp.dot(mb, upper, preferred_element_type=F32) + jnp.dot(before, ones, preferred_element_type=F32)
    words_ref[S:S + 8, :] = jnp.dot(every, ones, preferred_element_type=F32).astype(I32)
    rank_v[...] = jnp.where(mask, rank, -1.0).astype(I32)
    base = jnp.where(mask, ((cc + HALF) >> 6) * rows + rr + patch, 0)
    word = base + ((cc & (LANES - 1)) << 14) + (plane(2).astype(I32) << 21)
    pieces = [(word & 255).astype(F32), ((word >> 8) & 255).astype(F32), ((word >> 16) & 255).astype(F32)]
    for t in range(taylor):
        rest = plane(3 + t)
        for _ in range(3):
            pieces.append(rest.astype(BF16).astype(F32))
            rest = rest - pieces[-1]
    for n, piece in enumerate(pieces):
        piece_v[n * S:(n + 1) * S, :] = piece
    srow = lax.broadcasted_iota(I32, (S, LANES), 0)

    def spread(d, got):
        rank = rank_v[pl.ds(d, 1), :]
        hit = (rank >> 7) == srow
        onehot = jnp.where((rank & (LANES - 1)) == i0, 1.0, 0.0).astype(BF16)
        lhs = jnp.concatenate([jnp.where(hit, piece_v[pl.ds(n * S + d, 1), :], 0.0) for n in range(len(pieces))], 0)
        return got + lax.dot_general(lhs.astype(BF16), onehot, (((1,), (1,)), ((), ())), preferred_element_type=F32)

    got = jnp.zeros((len(pieces) * S, LANES), F32)
    if S <= 16:
        for d in range(S):
            got = spread(d, got)
    else:
        got = lax.fori_loop(0, S, spread, got)
    part = [got[n * S:(n + 1) * S] for n in range(len(pieces))]
    words_ref[0:S, :] = part[0].astype(I32) + (part[1].astype(I32) << 8) + (part[2].astype(I32) << 16)
    for t in range(taylor):
        amps_ref[t * S:(t + 1) * S, :] = part[3 + 3 * t] + (part[4 + 3 * t] + part[5 + 3 * t])


def pairwise(terms):
    while len(terms) > 1:
        terms = [sum(terms[n + 1:n + 2], terms[n]) for n in range(0, len(terms), 2)]
    return terms[0]


def render_kernel(list_ref, psi_ref, g_ref, dirty_hbm, res_ref, tay_ref,
                  words_ref, amps_ref, piece_v, rank_v, gt_ref, words_s, amps_s, dirty_ref, acc, acct, sems, *,
                  patch, tile, taylor, scales, origin, shares, start):
    rows = tile + 2 * patch
    S = words_ref.shape[0] - 8
    h = patch // 2
    copies = (pltpu.make_async_copy(words_ref, words_s, sems.at[0]),
              pltpu.make_async_copy(amps_ref, amps_s, sems.at[1]),
              pltpu.make_async_copy(dirty_hbm, dirty_ref, sems.at[2]))
    copies[2].start()
    list_components(list_ref, words_ref, amps_ref, piece_v, rank_v,
                    patch=patch, tile=tile, taylor=taylor, origin=origin)
    copies[0].start()
    copies[1].start()
    pack_fit(psi_ref, gt_ref, patch=patch, shares=shares, start=start)
    for j in range(1, acc.shape[0] // rows - 1):
        acc[pl.ds(j * rows + patch, tile), :] = jnp.zeros((tile, LANES), F32)
        acct[pl.ds(j * rows + patch - h, tile + h), :] = jnp.zeros((tile + h, LANES), F32)
    for copy in copies[:2]:
        copy.wait()
    n = words_s[S, 0]
    lane_half = lax.broadcasted_iota(I32, (1, LANES), 1) & (HALF - 1)

    def gen(it, k):
        row, col = it // (LANES // U), (it % (LANES // U)) * U + k
        word = words_s[row, col]
        base, turn, width = word & 16383, (word >> 14) & (LANES - 1), word >> 21
        gb, hb = pl.multiple_of(width * patch, 8), pl.multiple_of(width * h, 8)
        ps, qs = [], []
        for t in range(taylor):
            a = amps_s[row + t * S, col]
            ps.append(a * g_ref[pl.ds(gb + t * scales * patch, patch), :])
            qs.append(a * gt_ref[pl.ds(hb + t * scales * h, h), :])
        p, q = pairwise(ps), pairwise(qs)
        p = p.astype(BF16).astype(F32)
        return pltpu.roll(p, turn, 1), pltpu.roll(q, turn, 1), base, turn & (HALF - 1)

    def put(p, q, base, turn):
        first = lane_half >= turn
        for ref, val, high in ((acc, p, patch), (acct, q, h)):
            here, right = pl.ds(base, high), pl.ds(base + rows, high)
            ref[here, :] = ref[here, :] + jnp.where(first, val, 0.0)
            ref[right, :] = ref[right, :] + jnp.where(first, 0.0, val)

    def step(i, carry):
        for item in [gen(i, k) for k in range(U)]:
            put(*item)
        return carry

    lax.fori_loop(0, (n + U - 1) // U, step, 0)

    copies[2].wait()
    left = lax.broadcasted_iota(I32, (tile, LANES), 1) < HALF
    for c in range(tile // LANES):
        j, cols = 2 * c + 1, slice(c * LANES, (c + 1) * LANES)

        def get(ref, jj, top):
            return ref[pl.ds(jj * rows + top, tile), :]

        x, y = get(acc, j, patch), get(acc, j + 1, patch)
        res_ref[0, :, cols] = dirty_ref[0, :, cols] - jnp.where(left, x, y)
        res_ref[1, :, cols] = dirty_ref[1, :, cols] - pltpu.roll(jnp.where(left, y, x), HALF, 1)
        up = jnp.where(left, get(acct, j, patch), get(acct, j + 1, patch))
        low = pltpu.roll(jnp.where(left, get(acct, j + 1, patch - h), get(acct, j, patch - h)), HALF, 1)
        tay_ref[0, :, cols] = up + low


def render(lists, psi, g, dirty, origin, start, *, patch, taylor, scales, shares):
    tile, S = dirty.shape[1], lists.shape[0] // LIST
    rows, tiles = tile + 2 * patch, tile // HALF + 2
    return pl.pallas_call(
        functools.partial(render_kernel, patch=patch, tile=tile, taylor=taylor, scales=scales,
                          origin=origin, shares=shares, start=start),
        out_shape=(jax.ShapeDtypeStruct(dirty.shape, F32), jax.ShapeDtypeStruct((1,) + dirty.shape[1:], F32)),
        in_specs=[vmem()] * 3 + [pl.BlockSpec(memory_space=pltpu.HBM)], out_specs=(vmem(),) * 2,
        scratch_shapes=[
            pltpu.VMEM((S + 8, LANES), I32), pltpu.VMEM((taylor * S, LANES), F32),
            pltpu.VMEM(((3 + 3 * taylor) * S, LANES), F32), pltpu.VMEM((S, LANES), I32),
            pltpu.VMEM((g.shape[0] // 2, LANES), F32),
            pltpu.SMEM((S + 8, LANES), I32), pltpu.SMEM((taylor * S, LANES), F32), pltpu.VMEM(dirty.shape, F32),
            pltpu.VMEM((tiles * rows, LANES), F32), pltpu.VMEM((tiles * rows, LANES), F32),
            pltpu.SemaphoreType.DMA((3,))],
        compiler_params=pltpu.CompilerParams(vmem_limit_bytes=12 * 1024 * 1024),
    )(lists, psi, g, pltpu.with_memory_space_constraint(dirty, pltpu.HBM))


def finish_kernel(res_ref, total_ref, fit_ref, res_hbm, tay_hbm, tay_ref, sems):
    bands = res_ref.shape[0]
    res = [pltpu.make_async_copy(res_ref.at[b], res_hbm.at[b], sems.at[1 + b]) for b in range(bands)]
    for copy in res:
        copy.start()
    tay_ref[...] = total_ref[...] - fit_ref[...]
    tay = pltpu.make_async_copy(tay_ref, tay_hbm, sems.at[0])
    tay.start()
    for copy in res:
        copy.wait()
    tay.wait()


def finish(residual, total, model_fit):
    return pl.pallas_call(
        finish_kernel,
        out_shape=(jax.ShapeDtypeStruct(residual.shape, F32), jax.ShapeDtypeStruct(total.shape, F32)),
        in_specs=[vmem()] * 3, out_specs=(pl.BlockSpec(memory_space=pltpu.HBM),) * 2,
        scratch_shapes=[pltpu.VMEM(total.shape, F32), pltpu.SemaphoreType.DMA((1 + residual.shape[0],))],
        compiler_params=pltpu.CompilerParams(vmem_limit_bytes=4 * 1024 * 1024),
    )(residual, total, model_fit)


def per_device(dirty, psf, comp_tile, comp_offset, comp_scale, comp_amp, fit_weight):
    bands, tile = dirty.shape[0], dirty.shape[1]
    patch = math.isqrt(psf.shape[2])
    taylor = comp_amp.shape[1]
    scales = psf.shape[1] // taylor
    n_ty, n_tx, n_band = lax.axis_size("ty"), lax.axis_size("tx"), lax.axis_size("band")
    lift = 2.0 ** math.floor(math.log2(65504.0 / (bands * 30.0)))
    bits = [1 << n for n in range((n_tx - 1).bit_length())]
    bits += [n_tx << n for n in range(1, (n_ty - 1).bit_length())] + [n_tx]
    shares = 2

    def share():
        return lax.axis_index("ty") % 2

    lists, psi_send, psi_keep, dirty_send, dirty_keep, pairs = prep(
        dirty, psf, comp_tile, comp_offset, comp_scale, comp_amp, fit_weight,
        lambda: lax.axis_index("band"), share, shares, n_tx, n_band, lift)

    def across(value, bit):
        got = lax.ppermute(value.astype(jnp.float16), "band", [(i, i ^ bit) for i in range(n_band)])
        return got.astype(F32) * (1.0 / lift)

    def hop(value, bit):
        return lax.ppermute(value, ("ty", "tx"), [(i, i ^ bit) for i in range(n_ty * n_tx)])

    psi = psi_keep + across(psi_send, 1)
    total = dirty_keep + across(dirty_send, 1)
    band_bits = [1 << n for n in range(1, (n_band - 1).bit_length())]
    for n, bit in enumerate(band_bits):
        cut = psi.shape[0] // 2
        got = across(psi[cut:] * lift, bit)
        psi = psi[:cut] + got
    g = pack(pairs, patch)
    for bit in bits[:-1]:
        lists = jnp.concatenate([lists, hop(lists, bit)], 0)
    cut = lists.shape[0]
    got = hop(jnp.concatenate([lists, psi[0]], 0), bits[-1])
    lists = jnp.concatenate([lists, got[:cut]], 0)
    psi = jnp.concatenate([psi[0], got[cut:]], 0)
    for bit in band_bits:
        cut = total.shape[0] // 2
        total = total[:cut] + across(total[cut:] * lift, bit)
    residual, model_fit = render(
        lists, psi, g, dirty, lambda: (lax.axis_index("ty") * tile, lax.axis_index("tx") * tile),
        lambda s: share() ^ s, patch=patch, taylor=taylor, scales=scales, shares=shares)
    return finish(residual, total, model_fit)


def solution(mesh):
    return jax.shard_map(
        per_device,
        mesh=mesh,
        in_specs=(
            P("band", "ty", "tx"),
            P("band", None, None),
            P(("ty", "tx"), None),
            P(("ty", "tx"), None),
            P(("ty", "tx")),
            P(("ty", "tx"), None),
            P("band", None),
        ),
        out_specs=(P("band", "ty", "tx"), P("band", "ty", "tx")),
        check_vma=False,
    )
```
